256 devices in a mesh: replica: 16 (over z_hi, x), fsdp: 16 (over y, z_lo, core).
Axes of the slice: x: 4, y: 4, z: 8 (z_hi: 4, z_lo: 2; z = z_hi * 2 + z_lo), core: 2. Of those that a mesh axis runs over, the one named last changes fastest.
Arguments:
- hidden: bfloat16 [32768, 4608], P(('replica', 'fsdp')), may hold values from -24 to 24
- key_cotangent: bfloat16 [32768, 1024], P(('replica', 'fsdp')), may hold values from -2 to 2
- norm_gain: float32 [4608], replicated, may hold values from 0.1 to 1.9
- weights: bfloat16 [16, 4, 4608, 1024], P('replica', None, 'fsdp'), may hold values from -0.796875 to 0.796875
- adam_first: float32 [16, 4608, 1024], P('replica', 'fsdp'), may hold values from -6 to 6
- adam_second: float32 [16, 4608, 1024], P('replica', 'fsdp'), may hold values from 0.5 to 50
- inner_step: int32 [], replicated, may hold values from 1 to 4096
- outer_global: float32 [4, 4608, 1024], P(None, 'fsdp', 'replica'), may hold values from -0.8 to 0.8
- outer_momentum: float32 [4, 4608, 1024], P(None, 'fsdp', 'replica'), may hold values from -0.8 to 0.8
Outputs:
- new_weights: bfloat16 [16, 4, 4608, 1024], P('replica', None, 'fsdp')
- hidden_grad: bfloat16 [32768, 4608], P(('replica', 'fsdp'))
- new_first: float32 [16, 4608, 1024], P('replica', 'fsdp')
- new_second: float32 [16, 4608, 1024], P('replica', 'fsdp')
- new_global: float32 [4, 4608, 1024], P(None, 'fsdp', 'replica')
- new_momentum: float32 [4, 4608, 1024], P(None, 'fsdp', 'replica')
The draws below stay inside these ranges and needn't reach their ends.
All inputs are finite; a program needn't handle non-finite values.
Results may differ from the reference program's by a relative error of at most 0.0006.
Values may be sent and summed in bfloat16 or wider, within the bound.
No kernel may reach another device: no remote copies, remote signals or barrier semaphores. Data moves between devices by JAX's collectives and lax.ppermute only.
A program may use at most 128 MiB of HBM per device.

```python
import math
import jax
import jax.numpy as jnp
from jax import lax

D = 4608
KV = 1024
FRAGS = 4
REP_TOKENS = 2048
TOKENS = 32768
N_REPLICA = 16


def raised(entries, own_key, source, target, blocks, factor):
    def block_of(position):
        return (jnp.arange(entries.shape[position]) // (entries.shape[position] // blocks)).reshape((-1,) + (1,) * (entries.ndim - 1 - position))

    first = jax.random.permutation(own_key, blocks)[block_of(target)]
    far = (block_of(target) + blocks // 2) % blocks
    return jnp.where((block_of(source) == first) | (block_of(source) == far), factor * entries, entries)


def levels(rng, extent, split, low, high):
    factor_of, own = 1.0, jax.random.fold_in(rng, 6)
    for position, blocks in split:
        steps = jnp.exp(jax.random.uniform(jax.random.fold_in(own, position), (blocks,), jnp.float32, low / len(split), high / len(split)))
        factor_of = factor_of * jnp.repeat(steps, extent[position] // blocks).reshape([-1 if axis == position else 1 for axis in range(len(extent))])
    return factor_of


def bell_draw(key, dims, width, limit, pieces=(), held_as=jnp.bfloat16):
    array = jax.random.normal(key, dims, jnp.float32) * width
    if len(pieces) > 0:
        array = levels(key, dims, pieces, -0.22, 0.18) * array
    return jnp.clip(array, min=-limit, max=limit).astype(held_as)


def gaussian_with(key, dims, spread, bound, split, heavy, held_as=jnp.bfloat16):
    drawn = spread * jax.random.normal(key, dims, jnp.float32)
    if split:
        drawn = drawn * levels(key, dims, split, -0.22, 0.18)
    return jnp.clip(raised(drawn, jax.random.fold_in(key, 3), *heavy), -bound, bound).astype(held_as)


def setup_inputs(seed: int = 0) -> dict:
    arg_keys = jax.random.split(jax.random.key(seed), 10)
    return {
        "hidden": gaussian_with(arg_keys[0], (TOKENS, D), 1.0, 24.0, ((0, 256),), (0, 1, 256, 6.0)),
        "key_cotangent": bell_draw(arg_keys[1], (TOKENS, KV), 0.25, 2.0, ((0, 256),)),
        "norm_gain": jnp.clip(1.0 + 0.18 * jax.random.normal(arg_keys[2], (D,), jnp.float32), 0.1, 1.9),
        "weights": gaussian_with(arg_keys[3], (N_REPLICA, FRAGS, D, KV), 0.1, 0.796875, ((0, 16), (2, 16)), (0, 3, 16, 2.0)),
        "adam_first": bell_draw(arg_keys[4], (N_REPLICA, D, KV), 1.0, 6.0, ((0, 16), (1, 16)), jnp.float32),
        "adam_second": jnp.clip(jnp.exp(math.log(50.0) - 4.6051702 * jax.random.uniform(arg_keys[5], (N_REPLICA, D, KV), jnp.float32) ** levels(arg_keys[5], (N_REPLICA, D, KV), ((0, 16), (1, 16)), -0.2, 0.2)), 0.5, 50.0),
        "inner_step": jax.random.randint(arg_keys[6], (), 1, 4097).astype(jnp.int32),
        "outer_global": bell_draw(arg_keys[7], (FRAGS, D, KV), 0.1, 0.8, ((1, 16), (2, 16)), jnp.float32),
        "outer_momentum": bell_draw(arg_keys[8], (FRAGS, D, KV), 0.1, 0.8, ((1, 16), (2, 16)), jnp.float32),
    }


beta_first = 0.9
beta_second = 0.95
inner_rate = 0.004
warmup_steps = 4096.0
weight_decay = 0.1
outer_rate = 0.7
outer_mom = 0.9
mix_share = 0.5
norm_eps = 1e-06
adam_eps = 1e-08

def reference(hidden, key_cotangent, norm_gain, weights, adam_first, adam_second, inner_step, outer_global, outer_momentum):
    frag_index = (inner_step % FRAGS).astype(jnp.int32)
    trained = lax.dynamic_index_in_dim(weights, frag_index, 1, keepdims=False)

    def replica_work(inputs):
        rows, cotan, local_w = inputs
        rows_f = rows.astype(jnp.float32)
        inverse = lax.rsqrt(lax.optimization_barrier(jnp.mean(rows_f * rows_f, axis=1, keepdims=True)) + norm_eps)
        normed = (rows_f * inverse * norm_gain).astype(jnp.bfloat16)
        grad = lax.dot_general(normed, cotan, (((0,), (0,)), ((), ())), preferred_element_type=jnp.float32)
        back = lax.dot_general(cotan, local_w, (((1,), (1,)), ((), ())), preferred_element_type=jnp.float32)
        scaled = norm_gain * back
        project = lax.optimization_barrier(jnp.mean(scaled * rows_f, axis=1, keepdims=True))
        grad_rows = (inverse * scaled - rows_f * inverse * inverse * inverse * project).astype(jnp.bfloat16)
        return (grad, grad_rows)
    grads, grad_rows = lax.map(replica_work, (hidden.reshape(N_REPLICA, REP_TOKENS, D), key_cotangent.reshape(N_REPLICA, REP_TOKENS, KV), trained))
    hidden_grad = grad_rows.reshape(TOKENS, D)
    counter = inner_step.astype(jnp.float32)
    step_rate = inner_rate * jnp.minimum(jnp.float32(1.0), counter / warmup_steps)
    new_first = beta_first * adam_first + (1.0 - beta_first) * grads
    new_second = beta_second * adam_second + (1.0 - beta_second) * grads * grads
    first_hat = new_first / (1.0 - jnp.power(jnp.float32(beta_first), counter))
    second_hat = new_second / (1.0 - jnp.power(jnp.float32(beta_second), counter))
    snapshot = trained.astype(jnp.float32)
    updated = snapshot - step_rate * (first_hat / (jnp.sqrt(second_hat) + adam_eps) + weight_decay * snapshot)
    total = lax.optimization_barrier(jnp.sum(snapshot, axis=0))
    glob_slot = lax.dynamic_index_in_dim(outer_global, frag_index, 0, keepdims=False)
    mom_slot = lax.dynamic_index_in_dim(outer_momentum, frag_index, 0, keepdims=False)
    pseudo = glob_slot - total / N_REPLICA
    momentum_next = outer_mom * mom_slot + pseudo
    global_next = glob_slot - outer_rate * (pseudo + outer_mom * momentum_next)
    merged = (mix_share * updated + (1.0 - mix_share) * global_next).astype(jnp.bfloat16)
    new_weights = lax.dynamic_update_index_in_dim(weights, merged, frag_index, 1)
    new_global = lax.dynamic_update_index_in_dim(outer_global, global_next, frag_index, 0)
    new_momentum = lax.dynamic_update_index_in_dim(outer_momentum, momentum_next, frag_index, 0)
    return (new_weights, hidden_grad, new_first, new_second, new_global, new_momentum)
```

```python
import jax
import jax.numpy as jnp
from jax import lax
from jax.sharding import PartitionSpec as P

FRAGS = 4


beta_first = 0.9
beta_second = 0.95
inner_rate = 0.004
warmup_steps = 4096.0
weight_decay = 0.1
outer_rate = 0.7
outer_mom = 0.9
mix_share = 0.5
norm_eps = 1e-06
adam_eps = 1e-08


def pack(share):
    rows, width = share.shape
    return share.reshape(2, rows // 2, width).transpose(1, 0, 2).reshape(rows // 2, 2 * width)


def unpack(packed):
    half, width = packed.shape
    return packed.reshape(half, 2, width // 2).transpose(1, 0, 2).reshape(2 * half, width // 2)


def local(
    hidden,
    key_cotangent,
    norm_gain,
    weights,
    adam_first,
    adam_second,
    inner_step,
    outer_global,
    outer_momentum,
):
    replicas = lax.axis_size("replica")
    shards = lax.axis_size("fsdp")
    tokens, width = hidden.shape
    rows = weights.shape[2]
    kv = weights.shape[3]
    share = kv // replicas
    frag_index = inner_step % FRAGS
    local_w = lax.dynamic_index_in_dim(weights[0], frag_index, 0, keepdims=False)
    glob_slot = lax.dynamic_index_in_dim(outer_global, frag_index, 0, keepdims=False)
    mom_slot = lax.dynamic_index_in_dim(outer_momentum, frag_index, 0, keepdims=False)

    cot_all = lax.all_gather(key_cotangent, "fsdp", axis=0)

    pieces = (
        local_w.reshape(2, rows // 2, replicas, share)
        .transpose(2, 1, 0, 3)
        .reshape(replicas, rows // 2, 2 * share)
    )
    pieces = lax.all_to_all(pieces, "replica", 0, 0, tiled=True)
    total = jnp.sum(pieces.astype(jnp.float32), axis=0)
    glob_packed = pack(glob_slot)
    pseudo = glob_packed - total / replicas
    momentum_packed = outer_mom * pack(mom_slot) + pseudo
    global_packed = glob_packed - outer_rate * (pseudo + outer_mom * momentum_packed)
    global_all = lax.all_gather(global_packed, "replica", axis=0)
    global_full = (
        global_all.reshape(replicas, rows // 2, 2, share)
        .transpose(2, 1, 0, 3)
        .reshape(rows, kv)
    )

    rows_f = hidden.astype(jnp.float32)
    inverse = lax.rsqrt(jnp.mean(rows_f * rows_f, axis=1, keepdims=True) + norm_eps)
    normed = (rows_f * inverse * norm_gain).astype(jnp.bfloat16)
    normed_t = normed.T.reshape(shards, rows, tokens)
    normed_t = lax.all_to_all(normed_t, "fsdp", 0, 0, tiled=True)
    grad = lax.dot_general(
        normed_t.transpose(1, 0, 2).reshape(rows, shards * tokens),
        cot_all.reshape(shards * tokens, kv),
        (((1,), (0,)), ((), ())),
        preferred_element_type=jnp.float32,
    )

    back_t = lax.dot_general(
        local_w,
        cot_all.reshape(shards * tokens, kv),
        (((1,), (1,)), ((), ())),
        preferred_element_type=jnp.float32,
    )
    back_t = back_t.reshape(rows, shards, tokens).transpose(1, 0, 2)
    back_t = lax.all_to_all(back_t, "fsdp", 0, 0, tiled=True)
    back = back_t.reshape(width, tokens).T
    scaled = norm_gain * back
    project = jnp.mean(scaled * rows_f, axis=1, keepdims=True)
    hidden_grad = (inverse * scaled - rows_f * inverse * inverse * inverse * project).astype(
        jnp.bfloat16
    )
    counter = inner_step.astype(jnp.float32)
    step_rate = inner_rate * jnp.minimum(jnp.float32(1.0), counter / warmup_steps)
    first_next = beta_first * adam_first[0] + (1.0 - beta_first) * grad
    second_next = beta_second * adam_second[0] + (1.0 - beta_second) * grad * grad
    first_hat = first_next / (1.0 - jnp.power(jnp.float32(beta_first), counter))
    second_hat = second_next / (1.0 - jnp.power(jnp.float32(beta_second), counter))
    snapshot = local_w.astype(jnp.float32)
    updated = snapshot - step_rate * (
        first_hat / (jnp.sqrt(second_hat) + adam_eps) + weight_decay * snapshot
    )
    merged = (mix_share * updated + (1.0 - mix_share) * global_full).astype(jnp.bfloat16)
    layers_out = lax.dynamic_update_index_in_dim(weights[0], merged, frag_index, 0)
    new_global = lax.dynamic_update_index_in_dim(
        outer_global, unpack(global_packed), frag_index, 0
    )
    new_momentum = lax.dynamic_update_index_in_dim(
        outer_momentum, unpack(momentum_packed), frag_index, 0
    )
    return (
        layers_out[None],
        hidden_grad,
        first_next[None],
        second_next[None],
        new_global,
        new_momentum,
    )


def solution(mesh):
    in_specs = (
        P(("replica", "fsdp"), None),
        P(("replica", "fsdp"), None),
        P(),
        P("replica", None, "fsdp", None),
        P("replica", "fsdp", None),
        P("replica", "fsdp", None),
        P(),
        P(None, "fsdp", "replica"),
        P(None, "fsdp", "replica"),
    )
    out_specs = (
        P("replica", None, "fsdp", None),
        P(("replica", "fsdp"), None),
        P("replica", "fsdp", None),
        P("replica", "fsdp", None),
        P(None, "fsdp", "replica"),
        P(None, "fsdp", "replica"),
    )
    return jax.shard_map(local, mesh=mesh, in_specs=in_specs, out_specs=out_specs, check_vma=False)
```

```python
import jax
import jax.numpy as jnp
from jax import lax
from jax.experimental import pallas as pl
from jax.experimental.pallas import tpu as pltpu
from jax.sharding import PartitionSpec as P

FRAGS = 4
NY = 4
NX = 4
NH = 4

beta_first = 0.9
beta_second = 0.95
inner_rate = 0.004
warmup_steps = 4096.0
weight_decay = 0.1
outer_rate = 0.7
outer_mom = 0.9
mix_share = 0.5
norm_eps = 1e-06
adam_eps = 1e-08

BF = jnp.bfloat16
F32 = jnp.float32
LIMIT = 60 * 1024 * 1024


def shape(dims, dtype):
    return jax.ShapeDtypeStruct(dims, dtype)


def whole(dims):
    return pl.BlockSpec(dims, lambda *_: (0,) * len(dims))


def call(kernel, name, outs, operands, scratch=(), flops=0):
    moved = sum(a.size * a.dtype.itemsize for a in tuple(operands[1:]) + tuple(outs))
    return pl.pallas_call(
        kernel,
        grid_spec=pltpu.PrefetchScalarGridSpec(
            num_scalar_prefetch=1,
            grid=(1,),
            in_specs=[whole(a.shape) for a in operands[1:]],
            out_specs=[whole(o.shape) for o in outs],
            scratch_shapes=list(scratch),
        ),
        out_shape=list(outs),
        compiler_params=pltpu.CompilerParams(vmem_limit_bytes=LIMIT),
        cost_estimate=pl.CostEstimate(flops=flops, bytes_accessed=moved, transcendentals=0),
        name=name,
    )(*operands)


def fsdp_move(array, dz, dc):
    return lax.ppermute(array, "fsdp", [(i, i ^ (dz * 2 + dc)) for i in range(4 * NY)])


def fsdp_trade(array, over_z):
    if over_z:
        groups = [[i * 2 + c for i in range(2 * NY)] for c in range(2)]
    else:
        groups = [[y * 4 + i for y in range(NY)] for i in range(4)]
    return lax.all_to_all(array, "fsdp", 0, 0, axis_index_groups=groups, tiled=True)


def replica_move(array, dh):
    pairs = [(i, (i // NX + dh) % NH * NX + i % NX) for i in range(NH * NX)]
    return lax.ppermute(array, "replica", pairs)


def replica_trade(array):
    groups = [[h * NX + x for x in range(NX)] for h in range(NH)]
    return lax.all_to_all(array, "replica", 0, 0, axis_index_groups=groups, tiled=True)


def lane_half(block_shape):
    return lax.broadcasted_iota(jnp.int32, block_shape, 1) < 64


def pick_kernel(pos, w_ref, slot_ref, out):
    slot_ref[...] = w_ref[0]
    half = w_ref.shape[1] // 2
    left = lane_half((half, 128))
    for q in range(w_ref.shape[2] // 128):
        block = w_ref[0, :, q * 128 : (q + 1) * 128].astype(F32)
        top, bottom = block[:half], block[half:]
        h, x = 2 * q // NX, 2 * q % NX
        out[x, h] = jnp.where(left, top, pltpu.roll(bottom, 64, 1)).astype(BF)
        out[x + 1, h] = jnp.where(left, pltpu.roll(top, 64, 1), bottom).astype(BF)


def pick(pos, weights):
    _, rows, kv = weights.shape
    piece = (NX, NH, rows // 2, 128)
    return pl.pallas_call(
        pick_kernel,
        grid_spec=pltpu.PrefetchScalarGridSpec(
            num_scalar_prefetch=1,
            grid=(1,),
            in_specs=[pl.BlockSpec((1, rows, kv), lambda i, pos: (pos[0], 0, 0))],
            out_specs=[whole((rows, kv)), whole(piece)],
        ),
        out_shape=[shape((rows, kv), BF), shape(piece, BF)],
        compiler_params=pltpu.CompilerParams(vmem_limit_bytes=LIMIT),
        cost_estimate=pl.CostEstimate(flops=0, bytes_accessed=6 * rows * kv, transcendentals=0),
        name="pick",
    )(pos, weights)


def keep_kernel(w_ref, out):
    out[...] = w_ref[...]


def keep(weights):
    block = pl.BlockSpec((1,) + weights.shape[1:], lambda i: (i, 0, 0))
    return pl.pallas_call(
        keep_kernel,
        grid=(weights.shape[0],),
        in_specs=[block],
        out_specs=block,
        out_shape=shape(weights.shape, BF),
        compiler_params=pltpu.CompilerParams(vmem_limit_bytes=LIMIT),
        cost_estimate=pl.CostEstimate(flops=0, bytes_accessed=4 * weights.size, transcendentals=0),
        name="keep",
    )(weights)


def sum_x_kernel(pos, pieces, *outs):
    for k in range(NH):
        h = lax.rem(pos[2] + k, NH)
        a, b, c, d = (pieces[x, h].astype(F32) for x in range(NX))
        outs[k][...] = (a + b) + (c + d)


def outer_kernel(pos, a, b, c, d, glob, mom, new_glob, new_mom, sent):
    frag = pos[0]
    total = ((a[...] + b[...]) + (c[...] + d[...])).T
    total = jnp.concatenate([total[:64], total[64:]], axis=1)
    new_glob[...] = glob[...]
    new_mom[...] = mom[...]
    slot = glob[frag]
    pseudo = slot - total / (NX * NH)
    momentum = outer_mom * mom[frag] + pseudo
    updated = slot - outer_rate * (pseudo + outer_mom * momentum)
    new_glob[frag] = updated
    new_mom[frag] = momentum
    half = total.shape[1] // 2
    sent[...] = jnp.concatenate([updated[:, :half], updated[:, half:]], axis=0).T


def stack_kernel(pos, a, b, c, d, out):
    for k, piece in enumerate((a, b, c, d)):
        h = lax.rem(pos[2] + NH - k, NH)
        for x in range(NX):
            out[x, h] = piece[...]


def norm_kernel(pos, hidden, gain, out, inv_out):
    width = hidden.shape[1]
    total = jnp.zeros((hidden.shape[0], 128), F32)
    for j in range(width // 128):
        block = hidden[:, j * 128 : (j + 1) * 128].astype(F32)
        total = total + block * block
    mean = jnp.sum(total, axis=1, keepdims=True) / width
    inverse = lax.rsqrt(mean + norm_eps)
    inv_out[...] = jnp.broadcast_to(inverse, inv_out.shape)
    for j in range(width // 128):
        at = slice(j * 128, (j + 1) * 128)
        block = hidden[:, at].astype(F32) * inverse * gain[:, at]
        out[at, :] = block.T.astype(BF)


def back_kernel(pos, w0, wz, wc, wzc, cots, out, turned):
    rows, depth = w0.shape
    tokens = cots.shape[1]
    for y in range(NY):
        for j in range(depth // 128):
            at = slice(j * 128, (j + 1) * 128)
            turned[at, y * tokens : (y + 1) * tokens] = cots[y, :, at].T
    for pair in range(NY // 2):
        cot = turned[:, 2 * pair * tokens : (2 * pair + 2) * tokens]
        for dz, dc, w in ((0, 0, w0), (0, 1, wc), (1, 0, wz), (1, 1, wzc)):
            start = (jnp.bitwise_xor(pos[4], dz) * 2 + jnp.bitwise_xor(pos[5], dc)) * rows
            at = pl.ds(pl.multiple_of(start, 32), rows)
            both = jnp.dot(w[...], cot, preferred_element_type=F32)
            out[2 * pair, at, :] = both[:, :tokens]
            out[2 * pair + 1, at, :] = both[:, tokens:]


def hidden_kernel(pos, hidden, gain, inv, backs, out, scratch):
    width = hidden.shape[1]
    total = jnp.zeros((hidden.shape[0], 128), F32)
    for j in range(width // 128):
        at = slice(j * 128, (j + 1) * 128)
        scaled = gain[:, at] * backs[at, :].T
        total = total + scaled * hidden[:, at].astype(F32)
        scratch[:, at] = scaled
    project = jnp.sum(total, axis=1, keepdims=True) / width
    inverse = inv[...]
    factor = inverse * inverse * inverse * project
    for j in range(width // 128):
        at = slice(j * 128, (j + 1) * 128)
        out[:, at] = (inverse * scratch[:, at] - hidden[:, at].astype(F32) * factor).astype(BF)


def token_sum(pos, normed, cots, cots_z, start, rows, at):
    left = [normed[2 * y + pos[4], pl.ds(start, rows), :] for y in range(NY)]
    left += [normed[2 * y + 1 - pos[4], pl.ds(start, rows), :] for y in range(NY)]
    right = [cots[y, :, at] for y in range(NY)] + [cots_z[y, :, at] for y in range(NY)]
    return jnp.dot(
        jnp.concatenate(left, axis=1), jnp.concatenate(right, axis=0), preferred_element_type=F32
    )


def other_kernel(pos, normed, cots, cots_z, out):
    rows, kv = out.shape
    start = pl.multiple_of((1 - pos[5]) * rows, 16)
    for j in range(kv // 256):
        at = slice(j * 256, (j + 1) * 256)
        out[:, at] = token_sum(pos, normed, cots, cots_z, start, rows, at)


def adam_kernel(
    pos, rates, normed, cots, cots_z, theirs, slot, first, second, shares, _, out, first_out, second_out
):
    rows = theirs.shape[0]
    half = rows // 2
    start = pl.multiple_of(pos[5] * rows, 16)
    grad = token_sum(pos, normed, cots, cots_z, start, rows, slice(None)) + theirs[...]
    first_next = beta_first * first[...] + (1.0 - beta_first) * grad
    second_next = beta_second * second[...] + (1.0 - beta_second) * grad * grad
    first_out[...] = first_next
    second_out[...] = second_next
    snapshot = slot[...].astype(F32)
    updated = snapshot - rates[0] * (
        (first_next / rates[1]) / (jnp.sqrt(second_next / rates[2]) + adam_eps)
        + weight_decay * snapshot
    )
    left = lane_half((half, 128))
    for x in range(0, NX, 2):
        at = slice(x * 64, x * 64 + 128)
        a, b = shares[x, 0], shares[x + 1, 0]
        top = jnp.where(left, a, pltpu.roll(b, 64, 1))
        bottom = jnp.where(left, pltpu.roll(a, 64, 1), b)
        out[0, :half, at] = (mix_share * updated[:half, at] + (1.0 - mix_share) * top).astype(BF)
        out[0, half:, at] = (mix_share * updated[half:, at] + (1.0 - mix_share) * bottom).astype(BF)


def adam(pos, rates, normed, cots, cots_z, theirs, slot, first, second, shares, weights):
    rows, kv = theirs.shape
    wide = kv // NH
    column = pl.BlockSpec((rows, wide), lambda i, *_: (0, i))
    cot_block = pl.BlockSpec(cots.shape[:2] + (wide,), lambda i, *_: (0, 0, i))
    share_block = pl.BlockSpec((NX, 1) + shares.shape[2:], lambda i, *_: (0, i, 0, 0))
    return pl.pallas_call(
        adam_kernel,
        grid_spec=pltpu.PrefetchScalarGridSpec(
            num_scalar_prefetch=2,
            grid=(NH,),
            in_specs=[whole(normed.shape), cot_block, cot_block]
            + [column] * 4
            + [share_block, pl.BlockSpec(memory_space=pl.ANY)],
            out_specs=[
                pl.BlockSpec((1, rows, wide), lambda i, pos, rates: (pos[0], 0, i)),
                column,
                column,
            ],
        ),
        out_shape=[shape(weights.shape, BF), shape((rows, kv), F32), shape((rows, kv), F32)],
        input_output_aliases={10: 0},
        compiler_params=pltpu.CompilerParams(vmem_limit_bytes=LIMIT),
        cost_estimate=pl.CostEstimate(
            flops=rows * kv * 2048, bytes_accessed=rows * kv * 28, transcendentals=0
        ),
        name="adam",
    )(pos, rates, normed, cots, cots_z, theirs, slot, first, second, shares, weights)


def local(
    hidden,
    key_cotangent,
    norm_gain,
    weights,
    adam_first,
    adam_second,
    inner_step,
    outer_global,
    outer_momentum,
):
    tokens, width = hidden.shape
    rows, kv = weights.shape[2:]
    frag_index = inner_step % FRAGS
    replica = lax.axis_index("replica")
    place = lax.axis_index("fsdp")
    pos = jnp.stack(
        [frag_index, replica % NX, replica // NX, place // 4, (place // 2) % 2, place % 2]
    ).astype(jnp.int32)
    counter = inner_step.astype(F32)
    rates = jnp.stack(
        [
            inner_rate * jnp.minimum(F32(1.0), counter / warmup_steps),
            1.0 - jnp.power(F32(beta_first), counter),
            1.0 - jnp.power(F32(beta_second), counter),
        ]
    )
    gain = norm_gain[None]

    cots = fsdp_trade(jnp.broadcast_to(key_cotangent[None], (NY, tokens, kv)), False)
    slot, pieces = pick(pos, weights[0])
    w_z = fsdp_move(slot, 1, 0)
    w_c = fsdp_move(slot, 0, 1)
    w_zc = fsdp_move(w_z, 0, 1)
    pieces = replica_trade(pieces)
    normed, inv = call(
        norm_kernel,
        "norm",
        [shape((width, tokens), BF), shape((tokens, 128), F32)],
        (pos, hidden, gain),
    )
    normed = fsdp_trade(normed.reshape(2 * NY, 2 * rows, tokens), True)

    (backs,) = call(
        back_kernel,
        "back_product",
        [shape((NY, 4 * rows, tokens), F32)],
        (pos, slot, w_z, w_c, w_zc, cots),
        scratch=[pltpu.VMEM((kv, NY * tokens), BF)],
        flops=2 * 4 * rows * kv * NY * tokens,
    )
    backs = fsdp_trade(backs, False).reshape(width, tokens)
    (hidden_grad,) = call(
        hidden_kernel,
        "hidden_back",
        [shape(hidden.shape, BF)],
        (pos, hidden, gain, inv, backs),
        scratch=[pltpu.VMEM(hidden.shape, F32)],
    )

    packed = shape((rows // 2, 128), F32)
    parts = call(sum_x_kernel, "sum_x", [packed] * NH, (pos, pieces))
    parts = [parts[0]] + [replica_move(parts[d], d) for d in range(1, NH)]
    turned = [jnp.swapaxes(a, 1, 2) for a in (outer_global, outer_momentum)]
    new_global, new_momentum, share = call(
        outer_kernel,
        "outer",
        [shape(turned[0].shape, F32), shape(turned[0].shape, F32), packed],
        (pos, *parts, *turned),
    )
    shares = [share] + [replica_move(share, d) for d in range(1, NH)]
    (shares,) = call(stack_kernel, "stack", [shape((NX, NH) + packed.shape, F32)], (pos, *shares))
    shares = replica_trade(shares)

    cots_z = fsdp_move(cots, 1, 0)
    (theirs,) = call(
        other_kernel,
        "other_half",
        [shape((rows, kv), F32)],
        (pos, normed, cots, cots_z),
        flops=rows * kv * 2048,
    )
    theirs = fsdp_move(theirs, 0, 1)
    layers_out, first_next, second_next = adam(
        pos,
        rates,
        normed,
        cots,
        cots_z,
        theirs,
        slot,
        adam_first[0],
        adam_second[0],
        shares,
        keep(weights[0]),
    )
    return (
        layers_out[None],
        hidden_grad,
        first_next[None],
        second_next[None],
        jnp.swapaxes(new_global, 1, 2),
        jnp.swapaxes(new_momentum, 1, 2),
    )


def solution(mesh):
    in_specs = (
        P(("replica", "fsdp"), None),
        P(("replica", "fsdp"), None),
        P(),
        P("replica", None, "fsdp", None),
        P("replica", "fsdp", None),
        P("replica", "fsdp", None),
        P(),
        P(None, "fsdp", "replica"),
        P(None, "fsdp", "replica"),
    )
    out_specs = (
        P("replica", None, "fsdp", None),
        P(("replica", "fsdp"), None),
        P("replica", "fsdp", None),
        P("replica", "fsdp", None),
        P(None, "fsdp", "replica"),
        P(None, "fsdp", "replica"),
    )
    return jax.shard_map(local, mesh=mesh, in_specs=in_specs, out_specs=out_specs, check_vma=False)
```

```python
import functools

import jax
import jax.numpy as jnp
from jax import lax
from jax.experimental import pallas as pl
from jax.experimental.pallas import tpu as pltpu
from jax.sharding import PartitionSpec as P

FRAGS = 4
NY = 4
NX = 4
NH = 4

beta_first = 0.9
beta_second = 0.95
inner_rate = 0.004
warmup_steps = 4096.0
weight_decay = 0.1
outer_rate = 0.7
outer_mom = 0.9
mix_share = 0.5
norm_eps = 1e-06
adam_eps = 1e-08

BF = jnp.bfloat16
F32 = jnp.float32
LIMIT = 20 * 1024 * 1024
MEAN_SHARE = outer_rate * (1.0 + outer_mom) / (NX * NH)


def shape(dims, dtype):
    return jax.ShapeDtypeStruct(dims, dtype)


def in_hbm(array):
    return pltpu.with_memory_space_constraint(array, pltpu.HBM)


def whole(dims):
    return pl.BlockSpec(dims, lambda *_: (0,) * len(dims))


def call(kernel, name, outs, operands, scratch=()):
    return pl.pallas_call(
        kernel,
        grid_spec=pltpu.PrefetchScalarGridSpec(
            num_scalar_prefetch=1,
            grid=(1,),
            in_specs=[whole(a.shape) for a in operands[1:]],
            out_specs=[whole(o.shape) for o in outs],
            scratch_shapes=list(scratch),
        ),
        out_shape=list(outs),
        compiler_params=pltpu.CompilerParams(vmem_limit_bytes=LIMIT),
        name=name,
    )(*operands)


def fsdp_move(array, dz, dc):
    return lax.ppermute(array, "fsdp", [(i, i ^ (dz * 2 + dc)) for i in range(4 * NY)])


def fsdp_trade(array):
    groups = [[y * 4 + i for y in range(NY)] for i in range(4)]
    return lax.all_to_all(array, "fsdp", 0, 0, axis_index_groups=groups, tiled=True)


def replica_turn(array, dx):
    pairs = [(i, i // NX * NX + (i % NX + dx) % NX) for i in range(NH * NX)]
    return lax.ppermute(array, "replica", pairs)


def replica_swap(array, step):
    pairs = []
    for replica in range(NH * NX):
        for place in range(4 * NY):
            flip = (1, 3)[(step + place) % 2]
            pairs.append((replica * 4 * NY + place, (replica ^ (flip * NX)) * 4 * NY + place))
    return lax.ppermute(array, ("replica", "fsdp"), pairs)


def after(pos, done):
    return lax.optimization_barrier((pos, done))


def lane_half(block_shape):
    return lax.broadcasted_iota(jnp.int32, block_shape, 1) < 64


def pick_kernel(pos, w_ref, slot_ref, *outs):
    outs, pieces = outs[:NX], outs[NX]
    slot_ref[...] = w_ref[0]
    half = w_ref.shape[1] // 2
    left = lane_half((half, 128))
    for q in range(w_ref.shape[2] // 128):
        block = w_ref[0, :, q * 128 : (q + 1) * 128].astype(F32)
        top, bottom = block[:half], block[half:]
        h, x = 2 * q // NX, 2 * q % NX
        pieces[x, h] = jnp.where(left, top, pltpu.roll(bottom, 64, 1)).astype(BF)
        pieces[x + 1, h] = jnp.where(left, pltpu.roll(top, 64, 1), bottom).astype(BF)
    for d in range(NX):
        outs[d][...] = pieces[lax.rem(pos[1] + d, NX)]


def pick(pos, weights):
    _, rows, kv = weights.shape
    piece = (NH, rows // 2, 128)
    return pl.pallas_call(
        pick_kernel,
        grid_spec=pltpu.PrefetchScalarGridSpec(
            num_scalar_prefetch=1,
            grid=(1,),
            in_specs=[pl.BlockSpec((1, rows, kv), lambda i, pos: (pos[0], 0, 0))],
            out_specs=[whole((rows, kv))] + [whole(piece)] * NX,
            scratch_shapes=[pltpu.VMEM((NX,) + piece, BF)],
        ),
        out_shape=[pltpu.HBM((rows, kv), BF)] + [shape(piece, BF)] * NX,
        compiler_params=pltpu.CompilerParams(vmem_limit_bytes=LIMIT),
        name="pick",
    )(pos, in_hbm(weights))


def keep_kernel(pos, w_ref, out):
    out[...] = w_ref[...]


def keep(pos, weights):
    block = pl.BlockSpec((1,) + weights.shape[1:], lambda i, pos: (i, 0, 0))
    return pl.pallas_call(
        keep_kernel,
        grid_spec=pltpu.PrefetchScalarGridSpec(
            num_scalar_prefetch=1,
            grid=(weights.shape[0],),
            in_specs=[block],
            out_specs=block,
        ),
        out_shape=shape(weights.shape, BF),
        compiler_params=pltpu.CompilerParams(vmem_limit_bytes=LIMIT),
        name="keep",
    )(pos, in_hbm(weights))


def stepped(slot, mom, mean):
    pseudo = slot - mean
    momentum = outer_mom * mom + pseudo
    return slot - outer_rate * (pseudo + outer_mom * momentum), momentum


def sum_x_kernel(pos, a, b, c, d, glob, mom, out):
    for h in range(NH):
        total = (a[h].astype(F32) + b[h].astype(F32)) + (c[h].astype(F32) + d[h].astype(F32))
        out[h] = MEAN_SHARE * total
    updated, _ = stepped(glob[pos[0]], mom[pos[0]], 0.0)
    half = updated.shape[1] // 2
    updated = jnp.concatenate([updated[:, :half], updated[:, half:]], axis=0).T
    out[pos[2]] = out[pos[2]] + updated


def pair_kernel(pos, a, b, out):
    out[...] = a[...] + b[...]


def outer_kernel(pos, totals, glob, mom, new_glob, new_mom):
    frag = pos[0]
    updated = totals[pos[2]].T
    updated = jnp.concatenate([updated[:64], updated[64:]], axis=1)
    new_glob[...] = glob[...]
    new_mom[...] = mom[...]
    new_glob[frag] = updated
    alone, _ = stepped(glob[frag], mom[frag], 0.0)
    mean = (updated - alone) / (outer_rate * (1.0 + outer_mom))
    new_mom[frag] = stepped(glob[frag], mom[frag], mean)[1]


def norm_kernel(pos, hidden, gain, cot, out, inv_out):
    tokens, width = hidden.shape
    chunk = width // NY
    total = jnp.zeros((tokens, 128), F32)
    for j in range(width // 128):
        block = hidden[:, j * 128 : (j + 1) * 128].astype(F32)
        total = total + block * block
    mean = jnp.sum(total, axis=1, keepdims=True) / width
    inverse = lax.rsqrt(mean + norm_eps)
    inv_out[...] = jnp.broadcast_to(inverse, inv_out.shape)
    for y in range(NY):
        for j in range(chunk // 128):
            at = slice(y * chunk + j * 128, y * chunk + (j + 1) * 128)
            block = hidden[:, at].astype(F32) * inverse * gain[at][None]
            out[y, j * 128 : (j + 1) * 128, :] = block.T.astype(BF)
        for j in range(cot.shape[1] // 128):
            at = slice(j * 128, (j + 1) * 128)
            out[y, chunk + j * tokens : chunk + (j + 1) * tokens, :] = cot[:, at]


def back_kernel(pos, w0, wz, wc, wzc, both, out, turned):
    rows, depth = w0.shape
    tokens = both.shape[2]
    for y in range(2):
        for j in range(depth // 128):
            cot = both[y, 4 * rows + j * tokens : 4 * rows + (j + 1) * tokens, :]
            turned[j * 128 : (j + 1) * 128, y * tokens : (y + 1) * tokens] = cot.T
    for dz, dc, w in ((0, 0, w0), (0, 1, wc), (1, 0, wz), (1, 1, wzc)):
        start = (jnp.bitwise_xor(pos[4], dz) * 2 + jnp.bitwise_xor(pos[5], dc)) * rows
        at = pl.ds(pl.multiple_of(start, 32), rows)
        product = jnp.dot(w[...], turned[...], preferred_element_type=F32)
        out[0, at, :] = product[:, :tokens]
        out[1, at, :] = product[:, tokens:]


def back_product(pos, weights, both):
    rows, kv = weights[0].shape
    tokens = both.shape[2]
    return pl.pallas_call(
        back_kernel,
        grid_spec=pltpu.PrefetchScalarGridSpec(
            num_scalar_prefetch=1,
            grid=(NY // 2,),
            in_specs=[whole((rows, kv))] * 4
            + [pl.BlockSpec((2,) + both.shape[1:], lambda i, pos: (i, 0, 0))],
            out_specs=pl.BlockSpec((2, 4 * rows, tokens), lambda i, pos: (i, 0, 0)),
            scratch_shapes=[pltpu.VMEM((kv, 2 * tokens), BF)],
        ),
        out_shape=pltpu.HBM((NY, 4 * rows, tokens), F32),
        compiler_params=pltpu.CompilerParams(vmem_limit_bytes=LIMIT),
        name="back_product",
    )(pos, *weights, both)


def grad_kernel(dz, pos, mine, theirs, out):
    rows, kv = out.shape
    tokens = mine.shape[2]
    start = (jnp.bitwise_xor(pos[4], dz) * 2 + pos[5]) * rows
    at = pl.ds(pl.multiple_of(start, 32), rows)
    left = jnp.concatenate([both[y, at, :] for both in (mine, theirs) for y in range(NY)], axis=1)
    for j in range(kv // 256):
        columns = []
        for b in (2 * j, 2 * j + 1):
            lines = slice(4 * rows + b * tokens, 4 * rows + (b + 1) * tokens)
            blocks = [both[y, lines, :] for both in (mine, theirs) for y in range(NY)]
            columns.append(jnp.concatenate(blocks, axis=0))
        out[:, j * 256 : (j + 1) * 256] = jnp.dot(
            left, jnp.concatenate(columns, axis=1), preferred_element_type=F32
        )


def hidden_kernel(pos, hidden, gain, inv, backs, out, scratch):
    width = hidden.shape[1]
    total = jnp.zeros((hidden.shape[0], 128), F32)
    for j in range(width // 128):
        at = slice(j * 128, (j + 1) * 128)
        scaled = gain[at][None] * backs[at, :].T
        total = total + scaled * hidden[:, at].astype(F32)
        scratch[:, at] = scaled
    project = jnp.sum(total, axis=1, keepdims=True) / width
    inverse = inv[...]
    factor = inverse * inverse * inverse * project
    for j in range(width // 128):
        at = slice(j * 128, (j + 1) * 128)
        out[:, at] = (inverse * scratch[:, at] - hidden[:, at].astype(F32) * factor).astype(BF)


def adam_kernel(pos, rates, own, far, slot, first, second, *refs):
    totals, (_, out, first_out, second_out, ordered) = refs[:NX], refs[NX:]
    for d in range(NX):
        ordered[lax.rem(pos[1] + NX - d, NX)] = totals[d][0]
    rows = own.shape[0]
    half = rows // 2
    grad = own[...] + far[...]
    first_next = beta_first * first[...] + (1.0 - beta_first) * grad
    second_next = beta_second * second[...] + (1.0 - beta_second) * grad * grad
    first_out[...] = first_next
    second_out[...] = second_next
    snapshot = slot[...].astype(F32)
    updated = snapshot - rates[0] * (
        (first_next / rates[1]) / (jnp.sqrt(second_next / rates[2]) + adam_eps)
        + weight_decay * snapshot
    )
    left = lane_half((half, 128))
    for x in range(0, NX, 2):
        at = slice(x * 64, x * 64 + 128)
        a, b = ordered[x], ordered[x + 1]
        top = jnp.where(left, a, pltpu.roll(b, 64, 1))
        bottom = jnp.where(left, pltpu.roll(a, 64, 1), b)
        out[0, :half, at] = (mix_share * updated[:half, at] + (1.0 - mix_share) * top).astype(BF)
        out[0, half:, at] = (mix_share * updated[half:, at] + (1.0 - mix_share) * bottom).astype(BF)


def adam(pos, rates, own, far, slot, first, second, totals, weights):
    rows, kv = own.shape
    wide = kv // NH
    column = pl.BlockSpec((rows, wide), lambda i, *_: (0, i))
    piece = totals[0].shape[1:]
    columns = [in_hbm(a) for a in (own, far, slot, first, second)]
    return pl.pallas_call(
        adam_kernel,
        grid_spec=pltpu.PrefetchScalarGridSpec(
            num_scalar_prefetch=2,
            grid=(NH,),
            in_specs=[column] * 5
            + [pl.BlockSpec((1,) + piece, lambda i, *_: (i, 0, 0))] * NX
            + [pl.BlockSpec(memory_space=pl.ANY)],
            out_specs=[
                pl.BlockSpec((1, rows, wide), lambda i, pos, rates: (pos[0], 0, i)),
                column,
                column,
            ],
            scratch_shapes=[pltpu.VMEM((NX,) + piece, F32)],
        ),
        out_shape=[shape(weights.shape, BF), shape((rows, kv), F32), shape((rows, kv), F32)],
        input_output_aliases={7 + NX: 0},
        compiler_params=pltpu.CompilerParams(vmem_limit_bytes=LIMIT),
        name="adam",
    )(pos, rates, *columns, *totals, weights)


def local(
    hidden,
    key_cotangent,
    norm_gain,
    weights,
    adam_first,
    adam_second,
    inner_step,
    outer_global,
    outer_momentum,
):
    tokens, width = hidden.shape
    rows, kv = weights.shape[2:]
    frag_index = inner_step % FRAGS
    replica = lax.axis_index("replica")
    place = lax.axis_index("fsdp")
    pos = jnp.stack(
        [frag_index, replica % NX, replica // NX, place // 4, (place // 2) % 2, place % 2]
    ).astype(jnp.int32)
    counter = inner_step.astype(F32)
    rates = jnp.stack(
        [
            inner_rate * jnp.minimum(F32(1.0), counter / warmup_steps),
            1.0 - jnp.power(F32(beta_first), counter),
            1.0 - jnp.power(F32(beta_second), counter),
        ]
    )
    gain = norm_gain

    both, inv = call(
        norm_kernel,
        "norm",
        [pltpu.HBM((NY, width // NY + kv, tokens), BF), pltpu.HBM((tokens, 128), F32)],
        (pos, hidden, gain, key_cotangent),
    )
    both = fsdp_trade(both)
    pos, inv = after(pos, inv)

    slot, *pieces = pick(pos, weights[0])
    w_z = fsdp_move(slot, 1, 0)
    pieces = [pieces[0]] + [replica_turn(pieces[d], d) for d in range(1, NX)]
    w_c = fsdp_move(slot, 0, 1)
    pos, slot = after(pos, slot)

    turned = [jnp.swapaxes(a, 1, 2) for a in (outer_global, outer_momentum)]
    packed = shape((NH, rows // 2, 128), F32)
    (totals,) = call(sum_x_kernel, "sum_x", [packed], (pos, *pieces, *turned))
    pos, totals = after(pos, totals)
    w_z, totals = after(w_z, totals)
    w_zc = fsdp_move(w_z, 0, 1)
    near_totals = replica_swap(totals, 0)
    (totals,) = call(pair_kernel, "sum_h", [packed], (pos, totals, near_totals))
    pos, totals = after(pos, totals)
    far_totals = replica_swap(totals, 1)
    pos, w_zc = after(pos, w_zc)

    both, totals = after(both, totals)
    both_c = fsdp_move(both, 0, 1)
    backs = back_product(pos, (slot, w_z, w_c, w_zc), both)
    pos, backs = after(pos, backs)
    backs = fsdp_trade(backs).reshape(width, tokens)

    (totals,) = call(pair_kernel, "sum_hh", [packed], (pos, totals, far_totals))
    pos, totals = after(pos, totals)
    all_totals = [totals] + [replica_turn(totals, d) for d in range(1, NX)]
    block = [pltpu.HBM((rows, kv), F32)]
    (far,) = call(functools.partial(grad_kernel, 1), "grad_far", block, (pos, both, both_c))
    pos, far = after(pos, far)
    far = fsdp_move(far, 1, 0)
    (own,) = call(functools.partial(grad_kernel, 0), "grad_near", block, (pos, both, both_c))
    pos, own = after(pos, own)

    new_global, new_momentum = call(
        outer_kernel, "outer", [shape(turned[0].shape, F32)] * 2, (pos, totals, *turned)
    )
    pos, new_global = after(pos, new_global)
    kept = keep(pos, weights[0])
    pos, kept = after(pos, kept)

    (hidden_grad,) = call(
        hidden_kernel,
        "hidden_back",
        [shape(hidden.shape, BF)],
        (pos, hidden, gain, inv, backs),
        scratch=[pltpu.VMEM(hidden.shape, F32)],
    )
    pos, hidden_grad = after(pos, hidden_grad)
    layers_out, first_next, second_next = adam(
        pos, rates, own, far, slot, adam_first[0], adam_second[0], all_totals, kept
    )
    return (
        layers_out[None],
        hidden_grad,
        first_next[None],
        second_next[None],
        jnp.swapaxes(new_global, 1, 2),
        jnp.swapaxes(new_momentum, 1, 2),
    )


def solution(mesh):
    in_specs = (
        P(("replica", "fsdp"), None),
        P(("replica", "fsdp"), None),
        P(),
        P("replica", None, "fsdp", None),
        P("replica", "fsdp", None),
        P("replica", "fsdp", None),
        P(),
        P(None, "fsdp", "replica"),
        P(None, "fsdp", "replica"),
    )
    out_specs = (
        P("replica", None, "fsdp", None),
        P(("replica", "fsdp"), None),
        P("replica", "fsdp", None),
        P("replica", "fsdp", None),
        P(None, "fsdp", "replica"),
        P(None, "fsdp", "replica"),
    )
    return jax.shard_map(local, mesh=mesh, in_specs=in_specs, out_specs=out_specs, check_vma=False)
```

```python
import functools

import jax
import jax.numpy as jnp
from jax import lax
from jax.experimental import pallas as pl
from jax.experimental.pallas import tpu as pltpu
from jax.sharding import PartitionSpec as P

FRAGS = 4
NY = 4
NX = 4
NH = 4

beta_first = 0.9
beta_second = 0.95
inner_rate = 0.004
warmup_steps = 4096.0
weight_decay = 0.1
outer_rate = 0.7
outer_mom = 0.9
mix_share = 0.5
norm_eps = 1e-06
adam_eps = 1e-08

BF = jnp.bfloat16
F32 = jnp.float32
LIMIT = 20 * 1024 * 1024
MEAN_SHARE = outer_rate * (1.0 + outer_mom) / (NX * NH)


def shape(dims, dtype):
    return jax.ShapeDtypeStruct(dims, dtype)


ANY = pl.BlockSpec(memory_space=pl.ANY)


def in_hbm(array):
    return pltpu.with_memory_space_constraint(array, pltpu.HBM)


def whole(dims):
    return pl.BlockSpec(dims, lambda *_: (0,) * len(dims))


def call(kernel, name, outs, operands, scratch=()):
    return pl.pallas_call(
        kernel,
        grid_spec=pltpu.PrefetchScalarGridSpec(
            num_scalar_prefetch=1,
            grid=(1,),
            in_specs=[whole(a.shape) for a in operands[1:]],
            out_specs=[whole(o.shape) for o in outs],
            scratch_shapes=list(scratch),
        ),
        out_shape=list(outs),
        compiler_params=pltpu.CompilerParams(vmem_limit_bytes=LIMIT),
        name=name,
    )(*operands)


def fsdp_move(array, dz, dc):
    return lax.ppermute(array, "fsdp", [(i, i ^ (dz * 2 + dc)) for i in range(4 * NY)])


def fsdp_trade(array):
    groups = [[y * 4 + i for y in range(NY)] for i in range(4)]
    return lax.all_to_all(array, "fsdp", 0, 0, axis_index_groups=groups, tiled=True)


def replica_turn(array, dx):
    pairs = [(i, i // NX * NX + (i % NX + dx) % NX) for i in range(NH * NX)]
    return lax.ppermute(array, "replica", pairs)


def replica_swap(array, step):
    pairs = []
    for replica in range(NH * NX):
        for place in range(4 * NY):
            flip = (1, 3)[(step + place) % 2]
            pairs.append((replica * 4 * NY + place, (replica ^ (flip * NX)) * 4 * NY + place))
    return lax.ppermute(array, ("replica", "fsdp"), pairs)


def after(pos, done):
    return lax.optimization_barrier((pos, done))


def lane_half(block_shape):
    return lax.broadcasted_iota(jnp.int32, block_shape, 1) < 64


def pick_kernel(pos, w_ref, slot_ref, *outs):
    outs, pieces = outs[:NX], outs[NX]
    slot_ref[...] = w_ref[0]
    half = w_ref.shape[1] // 2
    left = lane_half((half, 128))
    for q in range(w_ref.shape[2] // 128):
        block = w_ref[0, :, q * 128 : (q + 1) * 128].astype(F32)
        top, bottom = block[:half], block[half:]
        h, x = 2 * q // NX, 2 * q % NX
        pieces[x, h] = jnp.where(left, top, pltpu.roll(bottom, 64, 1)).astype(BF)
        pieces[x + 1, h] = jnp.where(left, pltpu.roll(top, 64, 1), bottom).astype(BF)
    for d in range(NX):
        outs[d][...] = pieces[lax.rem(pos[1] + d, NX)]


def pick(pos, weights):
    _, rows, kv = weights.shape
    piece = (NH, rows // 2, 128)
    return pl.pallas_call(
        pick_kernel,
        grid_spec=pltpu.PrefetchScalarGridSpec(
            num_scalar_prefetch=1,
            grid=(1,),
            in_specs=[pl.BlockSpec((1, rows, kv), lambda i, pos: (pos[0], 0, 0))],
            out_specs=[whole((rows, kv))] + [whole(piece)] * NX,
            scratch_shapes=[pltpu.VMEM((NX,) + piece, BF)],
        ),
        out_shape=[pltpu.HBM((rows, kv), BF)] + [shape(piece, BF)] * NX,
        compiler_params=pltpu.CompilerParams(vmem_limit_bytes=LIMIT),
        name="pick",
    )(pos, in_hbm(weights))


def keep_kernel(pos, w_ref, out):
    out[...] = w_ref[...]


def keep(pos, weights):
    block = pl.BlockSpec((1,) + weights.shape[1:], lambda i, pos: (i, 0, 0))
    return pl.pallas_call(
        keep_kernel,
        grid_spec=pltpu.PrefetchScalarGridSpec(
            num_scalar_prefetch=1,
            grid=(weights.shape[0],),
            in_specs=[block],
            out_specs=block,
        ),
        out_shape=shape(weights.shape, BF),
        compiler_params=pltpu.CompilerParams(vmem_limit_bytes=LIMIT),
        name="keep",
    )(pos, in_hbm(weights))


def stepped(slot, mom, mean):
    pseudo = slot - mean
    momentum = outer_mom * mom + pseudo
    return slot - outer_rate * (pseudo + outer_mom * momentum), momentum


def sum_x_kernel(pos, a, b, c, d, glob, mom, out):
    for h in range(NH):
        total = (a[h].astype(F32) + b[h].astype(F32)) + (c[h].astype(F32) + d[h].astype(F32))
        out[h] = MEAN_SHARE * total
    updated, _ = stepped(glob[pos[0]], mom[pos[0]], 0.0)
    half = updated.shape[1] // 2
    updated = jnp.concatenate([updated[:, :half], updated[:, half:]], axis=0).T
    out[pos[2]] = out[pos[2]] + updated


def pair_kernel(pos, a, b, out):
    out[...] = a[...] + b[...]


def outer_kernel(pos, totals, glob, mom, new_glob, new_mom):
    frag = pos[0]
    updated = totals[pos[2]].T
    updated = jnp.concatenate([updated[:64], updated[64:]], axis=1)
    new_glob[...] = glob[...]
    new_mom[...] = mom[...]
    new_glob[frag] = updated
    alone, _ = stepped(glob[frag], mom[frag], 0.0)
    mean = (updated - alone) / (outer_rate * (1.0 + outer_mom))
    new_mom[frag] = stepped(glob[frag], mom[frag], mean)[1]


def norm_kernel(pos, hidden, gain, cot, out, inv_out):
    tokens, width = hidden.shape
    chunk = width // NY
    total = jnp.zeros((tokens, 128), F32)
    for j in range(width // 128):
        block = hidden[:, j * 128 : (j + 1) * 128].astype(F32)
        total = total + block * block
    mean = jnp.sum(total, axis=1, keepdims=True) / width
    inverse = lax.rsqrt(mean + norm_eps)
    inv_out[...] = jnp.broadcast_to(inverse, inv_out.shape)
    for y in range(NY):
        for j in range(chunk // 128):
            at = slice(y * chunk + j * 128, y * chunk + (j + 1) * 128)
            block = hidden[:, at].astype(F32) * inverse * gain[at][None]
            out[y, j * 128 : (j + 1) * 128, :] = block.T.astype(BF)
        for j in range(cot.shape[1] // 128):
            at = slice(j * 128, (j + 1) * 128)
            out[y, chunk + j * tokens : chunk + (j + 1) * tokens, :] = cot[:, at]


def back_kernel(pos, w0, wz, wc, wzc, both, out, w_v, turned, out_v, in_sem, out_sem):
    rows, depth = w0.shape
    tokens = both.shape[2]
    loads = []
    for k, w in enumerate((w0, wc, wz, wzc)):
        loads.append(pltpu.make_async_copy(w, w_v.at[k], in_sem.at[k]))
        loads[k].start()
    for y in range(NY):
        for j in range(depth // 128):
            cot = both[y, 4 * rows + j * tokens : 4 * rows + (j + 1) * tokens, :]
            turned[j * 128 : (j + 1) * 128, y * tokens : (y + 1) * tokens] = cot.T
    stores = []
    for k, (dz, dc) in enumerate(((0, 0), (0, 1), (1, 0), (1, 1))):
        start = (jnp.bitwise_xor(pos[4], dz) * 2 + jnp.bitwise_xor(pos[5], dc)) * rows
        at = pl.ds(pl.multiple_of(start, 32), rows)
        loads[k].wait()
        for pair in range(NY // 2):
            cot = turned[:, 2 * pair * tokens : (2 * pair + 2) * tokens]
            product = jnp.dot(w_v[k], cot, preferred_element_type=F32)
            out_v[2 * pair, at, :] = product[:, :tokens]
            out_v[2 * pair + 1, at, :] = product[:, tokens:]
        stores.append(pltpu.make_async_copy(out_v.at[:, at, :], out.at[:, at, :], out_sem.at[k]))
        stores[k].start()
    for copy in stores:
        copy.wait()


def back_product(pos, weights, both):
    rows, kv = weights[0].shape
    tokens = both.shape[2]
    return pl.pallas_call(
        back_kernel,
        grid_spec=pltpu.PrefetchScalarGridSpec(
            num_scalar_prefetch=1,
            grid=(1,),
            in_specs=[ANY] * 4 + [pl.BlockSpec(memory_space=pltpu.VMEM)],
            out_specs=ANY,
            scratch_shapes=[
                pltpu.VMEM((4, rows, kv), BF),
                pltpu.VMEM((kv, NY * tokens), BF),
                pltpu.VMEM((NY, 4 * rows, tokens), F32),
                pltpu.SemaphoreType.DMA((4,)),
                pltpu.SemaphoreType.DMA((4,)),
            ],
        ),
        out_shape=pltpu.HBM((NY, 4 * rows, tokens), F32),
        compiler_params=pltpu.CompilerParams(vmem_limit_bytes=LIMIT),
        name="back_product",
    )(pos, *(in_hbm(w) for w in weights), both)


def grad_kernel(dz, begin, pos, mine, theirs, out):
    rows, wide = out.shape
    tokens = mine.shape[2]
    start = (jnp.bitwise_xor(pos[4], dz) * 2 + pos[5]) * rows
    at = pl.ds(pl.multiple_of(start, 32), rows)
    left = jnp.concatenate([both[y, at, :] for both in (mine, theirs) for y in range(NY)], axis=1)
    for j in range(wide // 256):
        columns = []
        for b in (begin // 128 + 2 * j, begin // 128 + 2 * j + 1):
            lines = slice(4 * rows + b * tokens, 4 * rows + (b + 1) * tokens)
            blocks = [both[y, lines, :] for both in (mine, theirs) for y in range(NY)]
            columns.append(jnp.concatenate(blocks, axis=0))
        out[:, j * 256 : (j + 1) * 256] = jnp.dot(
            left, jnp.concatenate(columns, axis=1), preferred_element_type=F32
        )


def grad_product(pos, both, both_c, dz, begin, shape_out, name):
    return pl.pallas_call(
        functools.partial(grad_kernel, dz, begin),
        grid_spec=pltpu.PrefetchScalarGridSpec(
            num_scalar_prefetch=1,
            grid=(1,),
            in_specs=[pl.BlockSpec(memory_space=pltpu.VMEM)] * 2,
            out_specs=whole(shape_out),
        ),
        out_shape=pltpu.HBM(shape_out, F32),
        compiler_params=pltpu.CompilerParams(vmem_limit_bytes=LIMIT),
        name=name,
    )(pos, both, both_c)


def hidden_kernel(pos, hidden, gain, inv, backs, out, scratch):
    width = hidden.shape[1]
    total = jnp.zeros((hidden.shape[0], 128), F32)
    for j in range(width // 128):
        at = slice(j * 128, (j + 1) * 128)
        scaled = gain[at][None] * backs[at, :].T
        total = total + scaled * hidden[:, at].astype(F32)
        scratch[:, at] = scaled
    project = jnp.sum(total, axis=1, keepdims=True) / width
    inverse = inv[...]
    factor = inverse * inverse * inverse * project
    for j in range(width // 128):
        at = slice(j * 128, (j + 1) * 128)
        out[:, at] = (inverse * scratch[:, at] - hidden[:, at].astype(F32) * factor).astype(BF)


def adam_kernel(pos, rates, own, far, slot, first, second, *refs):
    totals, (out, first_out, second_out, ordered) = refs[:NX], refs[-4:]
    for d in range(NX):
        ordered[lax.rem(pos[1] + NX - d, NX)] = totals[d][0]
    rows = own.shape[0]
    half = rows // 2
    grad = own[...] + far[...]
    first_next = beta_first * first[...] + (1.0 - beta_first) * grad
    second_next = beta_second * second[...] + (1.0 - beta_second) * grad * grad
    first_out[...] = first_next
    second_out[...] = second_next
    snapshot = slot[...].astype(F32)
    updated = snapshot - rates[0] * (
        (first_next * rates[1]) / (jnp.sqrt(second_next * rates[2]) + adam_eps)
        + weight_decay * snapshot
    )
    left = lane_half((half, 128))
    for x in range(0, NX, 2):
        at = slice(x * 64, x * 64 + 128)
        a, b = ordered[x], ordered[x + 1]
        top = jnp.where(left, a, pltpu.roll(b, 64, 1))
        bottom = jnp.where(left, pltpu.roll(a, 64, 1), b)
        out[0, :half, at] = (mix_share * updated[:half, at] + (1.0 - mix_share) * top).astype(BF)
        out[0, half:, at] = (mix_share * updated[half:, at] + (1.0 - mix_share) * bottom).astype(BF)


def adam(pos, rates, own, far, slot, first, second, totals, held, part):
    rows, kv = own.shape
    wide = kv // NH
    steps = NH // 2
    column = pl.BlockSpec((rows, wide), lambda i, *_: (0, steps * part + i))
    share_block = pl.BlockSpec((1,) + totals[0].shape[1:], lambda i, *_: (steps * part + i, 0, 0))
    columns = [in_hbm(a) for a in (own, far, slot, first, second)]
    in_specs = [column] * 5 + [share_block] * NX + [pl.BlockSpec(memory_space=pl.ANY)] * len(held)
    in_specs[1] = pl.BlockSpec((rows, wide), lambda i, *_: (0, i))
    return pl.pallas_call(
        adam_kernel,
        grid_spec=pltpu.PrefetchScalarGridSpec(
            num_scalar_prefetch=2,
            grid=(steps,),
            in_specs=in_specs,
            out_specs=[
                pl.BlockSpec((1, rows, wide), lambda i, pos, rates: (pos[0], 0, steps * part + i)),
                column,
                column,
            ],
            scratch_shapes=[pltpu.VMEM((NX,) + totals[0].shape[1:], F32)],
        ),
        out_shape=[shape(held[0].shape, BF), shape((rows, kv), F32), shape((rows, kv), F32)],
        input_output_aliases={7 + NX + k: k for k in range(len(held))},
        compiler_params=pltpu.CompilerParams(vmem_limit_bytes=LIMIT),
        name="adam",
    )(pos, rates, *columns, *totals, *held)


def local(
    hidden,
    key_cotangent,
    norm_gain,
    weights,
    adam_first,
    adam_second,
    inner_step,
    outer_global,
    outer_momentum,
):
    tokens, width = hidden.shape
    rows, kv = weights.shape[2:]
    frag_index = inner_step % FRAGS
    replica = lax.axis_index("replica")
    place = lax.axis_index("fsdp")
    pos = jnp.stack(
        [frag_index, replica % NX, replica // NX, place // 4, (place // 2) % 2, place % 2]
    ).astype(jnp.int32)
    counter = inner_step.astype(F32)
    rates = jnp.stack(
        [
            inner_rate * jnp.minimum(F32(1.0), counter / warmup_steps),
            1.0 / (1.0 - jnp.power(F32(beta_first), counter)),
            1.0 / (1.0 - jnp.power(F32(beta_second), counter)),
        ]
    )
    gain = norm_gain

    both, inv = call(
        norm_kernel,
        "norm",
        [pltpu.HBM((NY, width // NY + kv, tokens), BF), pltpu.HBM((tokens, 128), F32)],
        (pos, *(in_hbm(a) for a in (hidden, gain, key_cotangent))),
    )
    both = fsdp_trade(both)
    pos, inv = after(pos, inv)

    slot, *pieces = pick(pos, weights[0])
    w_z = fsdp_move(slot, 1, 0)
    pieces = [pieces[0]] + [replica_turn(pieces[d], d) for d in range(1, NX)]
    w_c = fsdp_move(slot, 0, 1)
    pos, slot = after(pos, slot)

    turned = [jnp.swapaxes(a, 1, 2) for a in (outer_global, outer_momentum)]
    packed = shape((NH, rows // 2, 128), F32)
    (totals,) = call(sum_x_kernel, "sum_x", [packed], (pos, *pieces, *turned))
    pos, totals = after(pos, totals)
    near_totals = replica_swap(totals, 0)
    w_z, totals = after(w_z, totals)
    w_zc = fsdp_move(w_z, 0, 1)
    pos, w_c, w_zc = lax.optimization_barrier((pos, w_c, w_zc))
    kept = keep(pos, weights[0])
    pos, kept = after(pos, kept)
    (totals,) = call(pair_kernel, "sum_h", [packed], (pos, totals, near_totals))
    pos, totals = after(pos, totals)
    far_totals = replica_swap(totals, 1)

    both, totals = after(both, totals)
    both_c = fsdp_move(both, 0, 1)
    backs = back_product(pos, (slot, w_z, w_c, w_zc), both)
    pos, backs = after(pos, backs)

    far = []
    for part in range(2):
        sums = grad_product(pos, both, both_c, 1, part * kv // 2, (rows, kv // 2), "grad_far")
        pos, sums = after(pos, sums)
        if part == 0:
            (totals,) = call(pair_kernel, "sum_hh", [packed], (pos, totals, far_totals))
            pos, totals, backs = lax.optimization_barrier((pos, totals, backs))
            backs = fsdp_trade(backs).reshape(width, tokens)
        sums, totals = after(sums, totals)
        far.append(fsdp_move(sums, 1, 0))
    all_totals = [totals] + [replica_turn(totals, d) for d in range(1, NX)]
    own = grad_product(pos, both, both_c, 0, 0, (rows, kv), "grad_near")
    pos, own = after(pos, own)

    new_global, new_momentum = call(
        outer_kernel, "outer", [shape(turned[0].shape, F32)] * 2, (pos, totals, *turned)
    )
    pos, new_global = after(pos, new_global)
    held = (kept,)
    for part in range(2):
        held = adam(
            pos, rates, own, far[part], slot, adam_first[0], adam_second[0], all_totals, held, part
        )
    layers_out, first_next, second_next = held
    pos, first_next = after(pos, first_next)
    (hidden_grad,) = call(
        hidden_kernel,
        "hidden_back",
        [shape(hidden.shape, BF)],
        (pos, hidden, gain, inv, backs),
        scratch=[pltpu.VMEM(hidden.shape, F32)],
    )
    return (
        layers_out[None],
        hidden_grad,
        first_next[None],
        second_next[None],
        jnp.swapaxes(new_global, 1, 2),
        jnp.swapaxes(new_momentum, 1, 2),
    )


def solution(mesh):
    in_specs = (
        P(("replica", "fsdp"), None),
        P(("replica", "fsdp"), None),
        P(),
        P("replica", None, "fsdp", None),
        P("replica", "fsdp", None),
        P("replica", "fsdp", None),
        P(),
        P(None, "fsdp", "replica"),
        P(None, "fsdp", "replica"),
    )
    out_specs = (
        P("replica", None, "fsdp", None),
        P(("replica", "fsdp"), None),
        P("replica", "fsdp", None),
        P("replica", "fsdp", None),
        P(None, "fsdp", "replica"),
        P(None, "fsdp", "replica"),
    )
    return jax.shard_map(local, mesh=mesh, in_specs=in_specs, out_specs=out_specs, check_vma=False)
```

```python
import functools

import jax
import jax.numpy as jnp
from jax import lax
from jax.experimental import pallas as pl
from jax.experimental.pallas import tpu as pltpu
from jax.sharding import PartitionSpec as P

FRAGS = 4
NY = 4
NX = 4
NH = 4

beta_first = 0.9
beta_second = 0.95
inner_rate = 0.004
warmup_steps = 4096.0
weight_decay = 0.1
outer_rate = 0.7
outer_mom = 0.9
mix_share = 0.5
norm_eps = 1e-06
adam_eps = 1e-08

BF = jnp.bfloat16
F32 = jnp.float32
LIMIT = 20 * 1024 * 1024
MEAN_SHARE = outer_rate * (1.0 + outer_mom) / (NX * NH)


def shape(dims, dtype):
    return jax.ShapeDtypeStruct(dims, dtype)


ANY = pl.BlockSpec(memory_space=pl.ANY)


def in_hbm(array):
    return pltpu.with_memory_space_constraint(array, pltpu.HBM)


def whole(dims):
    return pl.BlockSpec(dims, lambda *_: (0,) * len(dims))


def call(kernel, name, outs, operands, scratch=()):
    return pl.pallas_call(
        kernel,
        grid_spec=pltpu.PrefetchScalarGridSpec(
            num_scalar_prefetch=1,
            grid=(1,),
            in_specs=[whole(a.shape) for a in operands[1:]],
            out_specs=[whole(o.shape) for o in outs],
            scratch_shapes=list(scratch),
        ),
        out_shape=list(outs),
        compiler_params=pltpu.CompilerParams(vmem_limit_bytes=LIMIT),
        name=name,
    )(*operands)


def fsdp_move(array, dz, dc):
    return lax.ppermute(array, "fsdp", [(i, i ^ (dz * 2 + dc)) for i in range(4 * NY)])


def fsdp_trade(array):
    groups = [[y * 4 + i for y in range(NY)] for i in range(4)]
    return lax.all_to_all(array, "fsdp", 0, 0, axis_index_groups=groups, tiled=True)


def replica_turn(array, dx):
    pairs = [(i, i // NX * NX + (i % NX + dx) % NX) for i in range(NH * NX)]
    return lax.ppermute(array, "replica", pairs)


def replica_swap(array, step):
    pairs = []
    for replica in range(NH * NX):
        for place in range(4 * NY):
            flip = (1, 3)[(step + place) % 2]
            pairs.append((replica * 4 * NY + place, (replica ^ (flip * NX)) * 4 * NY + place))
    return lax.ppermute(array, ("replica", "fsdp"), pairs)


def after(pos, done):
    return lax.optimization_barrier((pos, done))


def lane_half(block_shape):
    return lax.broadcasted_iota(jnp.int32, block_shape, 1) < 64


def pick_kernel(pos, w_ref, slot_ref, *outs):
    outs, pieces = outs[:NX], outs[NX]
    slot_ref[...] = w_ref[0]
    half = w_ref.shape[1] // 2
    left = lane_half((half, 128))
    for q in range(w_ref.shape[2] // 128):
        block = w_ref[0, :, q * 128 : (q + 1) * 128].astype(F32)
        top, bottom = block[:half], block[half:]
        h, x = 2 * q // NX, 2 * q % NX
        pieces[x, h] = jnp.where(left, top, pltpu.roll(bottom, 64, 1)).astype(BF)
        pieces[x + 1, h] = jnp.where(left, pltpu.roll(top, 64, 1), bottom).astype(BF)
    for d in range(NX):
        outs[d][...] = pieces[lax.rem(pos[1] + d, NX)]


def pick(pos, weights):
    _, rows, kv = weights.shape
    piece = (NH, rows // 2, 128)
    return pl.pallas_call(
        pick_kernel,
        grid_spec=pltpu.PrefetchScalarGridSpec(
            num_scalar_prefetch=1,
            grid=(1,),
            in_specs=[pl.BlockSpec((1, rows, kv), lambda i, pos: (pos[0], 0, 0))],
            out_specs=[whole((rows, kv))] + [whole(piece)] * NX,
            scratch_shapes=[pltpu.VMEM((NX,) + piece, BF)],
        ),
        out_shape=[pltpu.HBM((rows, kv), BF)] + [shape(piece, BF)] * NX,
        compiler_params=pltpu.CompilerParams(vmem_limit_bytes=LIMIT),
        name="pick",
    )(pos, in_hbm(weights))


def keep_kernel(pos, w_ref, out):
    out[...] = w_ref[...]


def keep(pos, weights):
    block = pl.BlockSpec((1,) + weights.shape[1:], lambda i, pos: (i, 0, 0))
    return pl.pallas_call(
        keep_kernel,
        grid_spec=pltpu.PrefetchScalarGridSpec(
            num_scalar_prefetch=1,
            grid=(weights.shape[0],),
            in_specs=[block],
            out_specs=block,
        ),
        out_shape=shape(weights.shape, BF),
        compiler_params=pltpu.CompilerParams(vmem_limit_bytes=LIMIT),
        name="keep",
    )(pos, in_hbm(weights))


def stepped(slot, mom, mean):
    pseudo = slot - mean
    momentum = outer_mom * mom + pseudo
    return slot - outer_rate * (pseudo + outer_mom * momentum), momentum


def sum_x_kernel(pos, a, b, c, d, glob, mom, out):
    for h in range(NH):
        total = (a[h].astype(F32) + b[h].astype(F32)) + (c[h].astype(F32) + d[h].astype(F32))
        out[h] = MEAN_SHARE * total
    updated, _ = stepped(glob[pos[0]], mom[pos[0]], 0.0)
    half = updated.shape[1] // 2
    updated = jnp.concatenate([updated[:, :half], updated[:, half:]], axis=0).T
    out[pos[2]] = out[pos[2]] + updated


def pair_kernel(pos, a, b, out):
    out[...] = a[...] + b[...]


def outer_kernel(pos, totals, glob, mom, new_glob, new_mom):
    frag = pos[0]
    updated = totals[pos[2]].T
    updated = jnp.concatenate([updated[:64], updated[64:]], axis=1)
    new_glob[...] = glob[...]
    new_mom[...] = mom[...]
    new_glob[frag] = updated
    alone, _ = stepped(glob[frag], mom[frag], 0.0)
    mean = (updated - alone) / (outer_rate * (1.0 + outer_mom))
    new_mom[frag] = stepped(glob[frag], mom[frag], mean)[1]


def norm_kernel(pos, hidden, gain, cot, out, inv_out):
    tokens, width = hidden.shape
    chunk = width // NY
    total = jnp.zeros((tokens, 128), F32)
    for j in range(width // 128):
        block = hidden[:, j * 128 : (j + 1) * 128].astype(F32)
        total = total + block * block
    mean = jnp.sum(total, axis=1, keepdims=True) / width
    inverse = lax.rsqrt(mean + norm_eps)
    inv_out[...] = jnp.broadcast_to(inverse, inv_out.shape)
    for y in range(NY):
        for j in range(chunk // 128):
            at = slice(y * chunk + j * 128, y * chunk + (j + 1) * 128)
            block = hidden[:, at].astype(F32) * inverse * gain[at][None]
            out[y, j * 128 : (j + 1) * 128, :] = block.T.astype(BF)
        for j in range(cot.shape[1] // 128):
            at = slice(j * 128, (j + 1) * 128)
            out[y, chunk + j * tokens : chunk + (j + 1) * tokens, :] = cot[:, at]


def back_kernel(pos, w0, wz, wc, wzc, both, out, w_v, turned, out_v, in_sem, out_sem):
    rows, depth = w0.shape
    tokens = both.shape[2]
    loads = []
    for k, w in enumerate((w0, wc, wz, wzc)):
        loads.append(pltpu.make_async_copy(w, w_v.at[k], in_sem.at[k]))
        loads[k].start()
    for y in range(NY):
        for j in range(depth // 128):
            cot = both[y, 4 * rows + j * tokens : 4 * rows + (j + 1) * tokens, :]
            turned[j * 128 : (j + 1) * 128, y * tokens : (y + 1) * tokens] = cot.T
    stores = []
    for k, (dz, dc) in enumerate(((0, 0), (0, 1), (1, 0), (1, 1))):
        start = (jnp.bitwise_xor(pos[4], dz) * 2 + jnp.bitwise_xor(pos[5], dc)) * rows
        at = pl.ds(pl.multiple_of(start, 32), rows)
        loads[k].wait()
        for pair in range(NY // 2):
            cot = turned[:, 2 * pair * tokens : (2 * pair + 2) * tokens]
            product = jnp.dot(w_v[k], cot, preferred_element_type=F32)
            out_v[2 * pair, at, :] = product[:, :tokens]
            out_v[2 * pair + 1, at, :] = product[:, tokens:]
        stores.append(pltpu.make_async_copy(out_v.at[:, at, :], out.at[:, at, :], out_sem.at[k]))
        stores[k].start()
    for copy in stores:
        copy.wait()


def back_product(pos, weights, both):
    rows, kv = weights[0].shape
    tokens = both.shape[2]
    return pl.pallas_call(
        back_kernel,
        grid_spec=pltpu.PrefetchScalarGridSpec(
            num_scalar_prefetch=1,
            grid=(1,),
            in_specs=[ANY] * 4 + [pl.BlockSpec(memory_space=pltpu.VMEM)],
            out_specs=ANY,
            scratch_shapes=[
                pltpu.VMEM((4, rows, kv), BF),
                pltpu.VMEM((kv, NY * tokens), BF),
                pltpu.VMEM((NY, 4 * rows, tokens), F32),
                pltpu.SemaphoreType.DMA((4,)),
                pltpu.SemaphoreType.DMA((4,)),
            ],
        ),
        out_shape=pltpu.HBM((NY, 4 * rows, tokens), F32),
        compiler_params=pltpu.CompilerParams(vmem_limit_bytes=LIMIT),
        name="back_product",
    )(pos, *(in_hbm(w) for w in weights), both)


def grad_kernel(dz, pos, mine, theirs, *outs):
    rows = outs[0].shape[0]
    tokens = mine.shape[2]
    start = (jnp.bitwise_xor(pos[4], dz) * 2 + pos[5]) * rows
    at = pl.ds(pl.multiple_of(start, 32), rows)
    left = jnp.concatenate([both[y, at, :] for both in (mine, theirs) for y in range(NY)], axis=1)
    b = 0
    for out in outs:
        for j in range(out.shape[1] // 256):
            columns = []
            for _ in range(2):
                lines = slice(4 * rows + b * tokens, 4 * rows + (b + 1) * tokens)
                blocks = [both[y, lines, :] for both in (mine, theirs) for y in range(NY)]
                columns.append(jnp.concatenate(blocks, axis=0))
                b += 1
            out[:, j * 256 : (j + 1) * 256] = jnp.dot(
                left, jnp.concatenate(columns, axis=1), preferred_element_type=F32
            )


def grad_product(pos, both, both_c, dz, rows, widths, name):
    return pl.pallas_call(
        functools.partial(grad_kernel, dz),
        grid_spec=pltpu.PrefetchScalarGridSpec(
            num_scalar_prefetch=1,
            grid=(1,),
            in_specs=[pl.BlockSpec(memory_space=pltpu.VMEM)] * 2,
            out_specs=[whole((rows, wide)) for wide in widths],
        ),
        out_shape=[pltpu.HBM((rows, wide), F32) for wide in widths],
        compiler_params=pltpu.CompilerParams(vmem_limit_bytes=LIMIT),
        name=name,
    )(pos, both, both_c)


def hidden_kernel(pos, hidden, gain, inv, backs, out, scratch):
    width = hidden.shape[1]
    total = jnp.zeros((hidden.shape[0], 128), F32)
    for j in range(width // 128):
        at = slice(j * 128, (j + 1) * 128)
        scaled = gain[at][None] * backs[at, :].T
        total = total + scaled * hidden[:, at].astype(F32)
        scratch[:, at] = scaled
    project = jnp.sum(total, axis=1, keepdims=True) / width
    inverse = inv[...]
    factor = inverse * inverse * inverse * project
    for j in range(width // 128):
        at = slice(j * 128, (j + 1) * 128)
        out[:, at] = (inverse * scratch[:, at] - hidden[:, at].astype(F32) * factor).astype(BF)


def adam_kernel(pos, rates, own, far, slot, first, second, *refs):
    totals, (out, first_out, second_out, ordered) = refs[:NX], refs[-4:]
    for d in range(NX):
        ordered[lax.rem(pos[1] + NX - d, NX)] = totals[d][0]
    rows = own.shape[0]
    half = rows // 2
    grad = own[...] + far[...]
    first_next = beta_first * first[...] + (1.0 - beta_first) * grad
    second_next = beta_second * second[...] + (1.0 - beta_second) * grad * grad
    first_out[...] = first_next
    second_out[...] = second_next
    snapshot = slot[...].astype(F32)
    updated = snapshot - rates[0] * (
        (first_next * rates[1]) / (jnp.sqrt(second_next * rates[2]) + adam_eps)
        + weight_decay * snapshot
    )
    left = lane_half((half, 128))
    for x in range(0, NX, 2):
        at = slice(x * 64, x * 64 + 128)
        a, b = ordered[x], ordered[x + 1]
        top = jnp.where(left, a, pltpu.roll(b, 64, 1))
        bottom = jnp.where(left, pltpu.roll(a, 64, 1), b)
        out[0, :half, at] = (mix_share * updated[:half, at] + (1.0 - mix_share) * top).astype(BF)
        out[0, half:, at] = (mix_share * updated[half:, at] + (1.0 - mix_share) * bottom).astype(BF)


def adam(pos, rates, own, far, slot, first, second, totals, held, begin):
    rows, kv = own.shape
    wide = kv // NH
    steps = far.shape[1] // wide
    skip = begin // wide
    column = pl.BlockSpec((rows, wide), lambda i, *_: (0, skip + i))
    share_block = pl.BlockSpec((1,) + totals[0].shape[1:], lambda i, *_: (skip + i, 0, 0))
    columns = [in_hbm(a) for a in (own, far, slot, first, second)]
    in_specs = [column] * 5 + [share_block] * NX + [pl.BlockSpec(memory_space=pl.ANY)] * len(held)
    in_specs[1] = pl.BlockSpec((rows, wide), lambda i, *_: (0, i))
    return pl.pallas_call(
        adam_kernel,
        grid_spec=pltpu.PrefetchScalarGridSpec(
            num_scalar_prefetch=2,
            grid=(steps,),
            in_specs=in_specs,
            out_specs=[
                pl.BlockSpec((1, rows, wide), lambda i, pos, rates: (pos[0], 0, skip + i)),
                column,
                column,
            ],
            scratch_shapes=[pltpu.VMEM((NX,) + totals[0].shape[1:], F32)],
        ),
        out_shape=[shape(held[0].shape, BF), shape((rows, kv), F32), shape((rows, kv), F32)],
        input_output_aliases={7 + NX + k: k for k in range(len(held))},
        compiler_params=pltpu.CompilerParams(vmem_limit_bytes=LIMIT),
        name="adam",
    )(pos, rates, *columns, *totals, *held)


def last_kernel(pos, rates, hidden, gain, inv, backs, own, far, slot, first, second, *refs):
    totals, (hidden_out, out, first_out, second_out, scratch, ordered) = refs[:NX], refs[-6:]
    hidden_kernel(pos, hidden, gain, inv, backs, hidden_out, scratch)
    wide = 64 * NX
    for k in range(own.shape[1] // wide):
        at = slice(k * wide, (k + 1) * wide)
        adam_kernel(
            pos,
            rates,
            *(a.at[:, at] for a in (own, far, slot, first, second)),
            *(t.at[k : k + 1] for t in totals),
            out.at[:, :, at],
            first_out.at[:, at],
            second_out.at[:, at],
            ordered,
        )


def last(pos, rates, hidden, gain, inv, backs, own, far, slot, first, second, totals, held):
    rows, kv = own.shape
    wide = far.shape[1]
    end = kv // wide - 1
    column = pl.BlockSpec((rows, wide), lambda *_: (0, end))
    share_block = pl.BlockSpec((NH * wide // kv,) + totals[0].shape[1:], lambda *_: (end, 0, 0))
    tokens = [in_hbm(a) for a in (hidden, gain, inv, backs)]
    columns = [in_hbm(a) for a in (own, far, slot, first, second)]
    return pl.pallas_call(
        last_kernel,
        grid_spec=pltpu.PrefetchScalarGridSpec(
            num_scalar_prefetch=2,
            grid=(1,),
            in_specs=[whole(a.shape) for a in tokens]
            + [column, whole(far.shape)]
            + [column] * 3
            + [share_block] * NX
            + [ANY] * 3,
            out_specs=[
                whole(hidden.shape),
                pl.BlockSpec((1, rows, wide), lambda i, pos, rates: (pos[0], 0, end)),
                column,
                column,
            ],
            scratch_shapes=[
                pltpu.VMEM(hidden.shape, F32),
                pltpu.VMEM((NX,) + totals[0].shape[1:], F32),
            ],
        ),
        out_shape=[shape(hidden.shape, BF)] + [shape(a.shape, a.dtype) for a in held],
        input_output_aliases={11 + NX + k: 1 + k for k in range(3)},
        compiler_params=pltpu.CompilerParams(vmem_limit_bytes=2 * LIMIT),
        name="last",
    )(pos, rates, *tokens, *columns, *totals, *held)


def local(
    hidden,
    key_cotangent,
    norm_gain,
    weights,
    adam_first,
    adam_second,
    inner_step,
    outer_global,
    outer_momentum,
):
    tokens, width = hidden.shape
    rows, kv = weights.shape[2:]
    frag_index = inner_step % FRAGS
    widths = [kv // 2, kv // 4, kv // 4]
    replica = lax.axis_index("replica")
    place = lax.axis_index("fsdp")
    pos = jnp.stack(
        [frag_index, replica % NX, replica // NX, place // 4, (place // 2) % 2, place % 2]
    ).astype(jnp.int32)
    counter = inner_step.astype(F32)
    rates = jnp.stack(
        [
            inner_rate * jnp.minimum(F32(1.0), counter / warmup_steps),
            1.0 / (1.0 - jnp.power(F32(beta_first), counter)),
            1.0 / (1.0 - jnp.power(F32(beta_second), counter)),
        ]
    )
    gain = norm_gain

    both, inv = call(
        norm_kernel,
        "norm",
        [pltpu.HBM((NY, width // NY + kv, tokens), BF), pltpu.HBM((tokens, 128), F32)],
        (pos, *(in_hbm(a) for a in (hidden, gain, key_cotangent))),
    )
    both = fsdp_trade(both)
    pos, inv = after(pos, inv)

    slot, *pieces = pick(pos, weights[0])
    w_z = fsdp_move(slot, 1, 0)
    pieces = [pieces[0]] + [replica_turn(pieces[d], d) for d in range(1, NX)]
    w_c = fsdp_move(slot, 0, 1)
    pos, slot = after(pos, slot)

    turned = [jnp.swapaxes(a, 1, 2) for a in (outer_global, outer_momentum)]
    packed = shape((NH, rows // 2, 128), F32)
    (totals,) = call(sum_x_kernel, "sum_x", [packed], (pos, *pieces, *turned))
    pos, totals = after(pos, totals)
    near_totals = replica_swap(totals, 0)
    w_z, totals = after(w_z, totals)
    w_zc = fsdp_move(w_z, 0, 1)
    pos, w_c, w_zc = lax.optimization_barrier((pos, w_c, w_zc))
    kept = keep(pos, weights[0])
    pos, kept = after(pos, kept)
    (totals,) = call(pair_kernel, "sum_h", [packed], (pos, totals, near_totals))
    pos, totals = after(pos, totals)
    far_totals = replica_swap(totals, 1)

    both, totals = after(both, totals)
    both_c = fsdp_move(both, 0, 1)
    backs = back_product(pos, (slot, w_z, w_c, w_zc), both)
    pos, backs = after(pos, backs)

    sums = grad_product(pos, both, both_c, 1, rows, widths, "grad_far")
    pos, *sums = lax.optimization_barrier((pos, *sums))
    (totals,) = call(pair_kernel, "sum_hh", [packed], (pos, totals, far_totals))
    pos, totals, backs, *sums = lax.optimization_barrier((pos, totals, backs, *sums))
    backs = fsdp_trade(backs).reshape(width, tokens)
    far = [fsdp_move(part, 1, 0) for part in sums]
    all_totals = [totals] + [replica_turn(totals, d) for d in range(1, NX)]
    (own,) = grad_product(pos, both, both_c, 0, rows, [kv], "grad_near")
    pos, own = after(pos, own)

    new_global, new_momentum = call(
        outer_kernel, "outer", [shape(turned[0].shape, F32)] * 2, (pos, totals, *turned)
    )
    pos, new_global = after(pos, new_global)
    held, begin = (kept,), 0
    for part in far[:-1]:
        held = adam(
            pos, rates, own, part, slot, adam_first[0], adam_second[0], all_totals, held, begin
        )
        begin += part.shape[1]
    hidden_grad, layers_out, first_next, second_next = last(
        pos,
        rates,
        hidden,
        gain,
        inv,
        backs,
        own,
        far[-1],
        slot,
        adam_first[0],
        adam_second[0],
        all_totals,
        held,
    )
    return (
        layers_out[None],
        hidden_grad,
        first_next[None],
        second_next[None],
        jnp.swapaxes(new_global, 1, 2),
        jnp.swapaxes(new_momentum, 1, 2),
    )


def solution(mesh):
    in_specs = (
        P(("replica", "fsdp"), None),
        P(("replica", "fsdp"), None),
        P(),
        P("replica", None, "fsdp", None),
        P("replica", "fsdp", None),
        P("replica", "fsdp", None),
        P(),
        P(None, "fsdp", "replica"),
        P(None, "fsdp", "replica"),
    )
    out_specs = (
        P("replica", None, "fsdp", None),
        P(("replica", "fsdp"), None),
        P("replica", "fsdp", None),
        P("replica", "fsdp", None),
        P(None, "fsdp", "replica"),
        P(None, "fsdp", "replica"),
    )
    return jax.shard_map(local, mesh=mesh, in_specs=in_specs, out_specs=out_specs, check_vma=False)
```

```python
import functools

import jax
import jax.numpy as jnp
from jax import lax
from jax.experimental import pallas as pl
from jax.experimental.pallas import tpu as pltpu
from jax.sharding import PartitionSpec as P

FRAGS = 4
NY = 4
NX = 4
NH = 4

beta_first = 0.9
beta_second = 0.95
inner_rate = 0.004
warmup_steps = 4096.0
weight_decay = 0.1
outer_rate = 0.7
outer_mom = 0.9
mix_share = 0.5
norm_eps = 1e-06
adam_eps = 1e-08

BF = jnp.bfloat16
F32 = jnp.float32
LIMIT = 20 * 1024 * 1024
MEAN_SHARE = outer_rate * (1.0 + outer_mom) / (NX * NH)


def shape(dims, dtype):
    return jax.ShapeDtypeStruct(dims, dtype)


ANY = pl.BlockSpec(memory_space=pl.ANY)


def in_hbm(array):
    return pltpu.with_memory_space_constraint(array, pltpu.HBM)


def whole(dims):
    return pl.BlockSpec(dims, lambda *_: (0,) * len(dims))


def call(kernel, name, outs, operands, scratch=()):
    return pl.pallas_call(
        kernel,
        grid_spec=pltpu.PrefetchScalarGridSpec(
            num_scalar_prefetch=1,
            grid=(1,),
            in_specs=[whole(a.shape) for a in operands[1:]],
            out_specs=[whole(o.shape) for o in outs],
            scratch_shapes=list(scratch),
        ),
        out_shape=list(outs),
        compiler_params=pltpu.CompilerParams(vmem_limit_bytes=LIMIT),
        name=name,
    )(*operands)


def fsdp_move(array, dz, dc):
    return lax.ppermute(array, "fsdp", [(i, i ^ (dz * 2 + dc)) for i in range(4 * NY)])


def fsdp_trade(array):
    groups = [[y * 4 + i for y in range(NY)] for i in range(4)]
    return lax.all_to_all(array, "fsdp", 0, 0, axis_index_groups=groups, tiled=True)


def replica_turn(array, dx):
    pairs = [(i, i // NX * NX + (i % NX + dx) % NX) for i in range(NH * NX)]
    return lax.ppermute(array, "replica", pairs)


def replica_swap(array, step):
    pairs = []
    for replica in range(NH * NX):
        for place in range(4 * NY):
            flip = (1, 3)[(step + place) % 2]
            pairs.append((replica * 4 * NY + place, (replica ^ (flip * NX)) * 4 * NY + place))
    return lax.ppermute(array, ("replica", "fsdp"), pairs)


def after(pos, done):
    return lax.optimization_barrier((pos, done))


def lane_half(block_shape):
    return lax.broadcasted_iota(jnp.int32, block_shape, 1) < 64


def pick_kernel(pos, w_ref, slot_ref, *outs):
    outs, pieces = outs[:NX], outs[NX]
    slot_ref[...] = w_ref[0]
    half = w_ref.shape[1] // 2
    left = lane_half((half, 128))
    for q in range(w_ref.shape[2] // 128):
        block = w_ref[0, :, q * 128 : (q + 1) * 128].astype(F32)
        top, bottom = block[:half], block[half:]
        h, x = 2 * q // NX, 2 * q % NX
        pieces[x, h] = jnp.where(left, top, pltpu.roll(bottom, 64, 1)).astype(BF)
        pieces[x + 1, h] = jnp.where(left, pltpu.roll(top, 64, 1), bottom).astype(BF)
    for d in range(NX):
        outs[d][...] = pieces[lax.rem(pos[1] + d, NX)]


def pick(pos, weights):
    _, rows, kv = weights.shape
    piece = (NH, rows // 2, 128)
    return pl.pallas_call(
        pick_kernel,
        grid_spec=pltpu.PrefetchScalarGridSpec(
            num_scalar_prefetch=1,
            grid=(1,),
            in_specs=[pl.BlockSpec((1, rows, kv), lambda i, pos: (pos[0], 0, 0))],
            out_specs=[whole((rows, kv))] + [whole(piece)] * NX,
            scratch_shapes=[pltpu.VMEM((NX,) + piece, BF)],
        ),
        out_shape=[shape((rows, kv), BF)] + [shape(piece, BF)] * NX,
        compiler_params=pltpu.CompilerParams(vmem_limit_bytes=LIMIT),
        name="pick",
    )(pos, in_hbm(weights))


def keep_kernel(pos, w_ref, out):
    out[...] = w_ref[...]


def keep(pos, weights):
    block = pl.BlockSpec((1,) + weights.shape[1:], lambda i, pos: (i, 0, 0))
    return pl.pallas_call(
        keep_kernel,
        grid_spec=pltpu.PrefetchScalarGridSpec(
            num_scalar_prefetch=1,
            grid=(weights.shape[0],),
            in_specs=[block],
            out_specs=block,
        ),
        out_shape=shape(weights.shape, BF),
        compiler_params=pltpu.CompilerParams(vmem_limit_bytes=LIMIT),
        name="keep",
    )(pos, in_hbm(weights))


def stepped(slot, mom, mean):
    pseudo = slot - mean
    momentum = outer_mom * mom + pseudo
    return slot - outer_rate * (pseudo + outer_mom * momentum), momentum


def sum_x_kernel(pos, a, b, c, d, glob, mom, out):
    for h in range(NH):
        total = (a[h].astype(F32) + b[h].astype(F32)) + (c[h].astype(F32) + d[h].astype(F32))
        out[h] = MEAN_SHARE * total
    updated, _ = stepped(glob[pos[0]], mom[pos[0]], 0.0)
    half = updated.shape[1] // 2
    updated = jnp.concatenate([updated[:, :half], updated[:, half:]], axis=0).T
    out[pos[2]] = out[pos[2]] + updated


def pair_kernel(pos, a, b, out):
    out[...] = a[...] + b[...]


def outer_kernel(pos, totals, glob, mom, new_glob, new_mom):
    frag = pos[0]
    updated = totals[pos[2]].T
    updated = jnp.concatenate([updated[:64], updated[64:]], axis=1)
    new_glob[...] = glob[...]
    new_mom[...] = mom[...]
    new_glob[frag] = updated
    alone, _ = stepped(glob[frag], mom[frag], 0.0)
    mean = (updated - alone) / (outer_rate * (1.0 + outer_mom))
    new_mom[frag] = stepped(glob[frag], mom[frag], mean)[1]


def norm_kernel(pos, hidden, gain, cot, out, inv_out):
    tokens, width = hidden.shape
    chunk = width // NY
    total = jnp.zeros((tokens, 128), F32)
    for j in range(width // 128):
        block = hidden[:, j * 128 : (j + 1) * 128].astype(F32)
        total = total + block * block
    mean = jnp.sum(total, axis=1, keepdims=True) / width
    inverse = lax.rsqrt(mean + norm_eps)
    inv_out[...] = jnp.broadcast_to(inverse, inv_out.shape)
    for y in range(NY):
        for j in range(chunk // 128):
            at = slice(y * chunk + j * 128, y * chunk + (j + 1) * 128)
            block = hidden[:, at].astype(F32) * inverse * gain[at][None]
            out[y, j * 128 : (j + 1) * 128, :] = block.T.astype(BF)
        for j in range(cot.shape[1] // 128):
            at = slice(j * 128, (j + 1) * 128)
            out[y, chunk + j * tokens : chunk + (j + 1) * tokens, :] = cot[:, at]


def back_kernel(pos, w0, wz, wc, wzc, both, out, w_v, turned, out_v, in_sem, out_sem):
    rows, depth = w0.shape
    tokens = both.shape[2]
    loads = []
    for k, w in enumerate((w0, wc, wz, wzc)):
        loads.append(pltpu.make_async_copy(w, w_v.at[k], in_sem.at[k]))
        loads[k].start()
    for y in range(NY):
        for j in range(depth // 128):
            cot = both[y, 4 * rows + j * tokens : 4 * rows + (j + 1) * tokens, :]
            turned[j * 128 : (j + 1) * 128, y * tokens : (y + 1) * tokens] = cot.T
    stores = []
    for k, (dz, dc) in enumerate(((0, 0), (0, 1), (1, 0), (1, 1))):
        start = (jnp.bitwise_xor(pos[4], dz) * 2 + jnp.bitwise_xor(pos[5], dc)) * rows
        at = pl.ds(pl.multiple_of(start, 32), rows)
        loads[k].wait()
        for pair in range(NY // 2):
            cot = turned[:, 2 * pair * tokens : (2 * pair + 2) * tokens]
            product = jnp.dot(w_v[k], cot, preferred_element_type=F32)
            out_v[2 * pair, at, :] = product[:, :tokens]
            out_v[2 * pair + 1, at, :] = product[:, tokens:]
        stores.append(pltpu.make_async_copy(out_v.at[:, at, :], out.at[:, at, :], out_sem.at[k]))
        stores[k].start()
    for copy in stores:
        copy.wait()


def back_product(pos, weights, both):
    rows, kv = weights[0].shape
    tokens = both.shape[2]
    return pl.pallas_call(
        back_kernel,
        grid_spec=pltpu.PrefetchScalarGridSpec(
            num_scalar_prefetch=1,
            grid=(1,),
            in_specs=[ANY] * 4 + [pl.BlockSpec(memory_space=pltpu.VMEM)],
            out_specs=ANY,
            scratch_shapes=[
                pltpu.VMEM((4, rows, kv), BF),
                pltpu.VMEM((kv, NY * tokens), BF),
                pltpu.VMEM((NY, 4 * rows, tokens), F32),
                pltpu.SemaphoreType.DMA((4,)),
                pltpu.SemaphoreType.DMA((4,)),
            ],
        ),
        out_shape=pltpu.HBM((NY, 4 * rows, tokens), F32),
        compiler_params=pltpu.CompilerParams(vmem_limit_bytes=LIMIT),
        name="back_product",
    )(pos, *(in_hbm(w) for w in weights), both)


def grad_kernel(dz, pos, mine, theirs, *outs):
    rows = outs[0].shape[0]
    tokens = mine.shape[2]
    start = (jnp.bitwise_xor(pos[4], dz) * 2 + pos[5]) * rows
    at = pl.ds(pl.multiple_of(start, 32), rows)
    left = jnp.concatenate([both[y, at, :] for both in (mine, theirs) for y in range(NY)], axis=1)
    b = 0
    for out in outs:
        for j in range(out.shape[1] // 256):
            columns = []
            for _ in range(2):
                lines = slice(4 * rows + b * tokens, 4 * rows + (b + 1) * tokens)
                blocks = [both[y, lines, :] for both in (mine, theirs) for y in range(NY)]
                columns.append(jnp.concatenate(blocks, axis=0))
                b += 1
            out[:, j * 256 : (j + 1) * 256] = jnp.dot(
                left, jnp.concatenate(columns, axis=1), preferred_element_type=F32
            )


def grad_product(pos, both, both_c, dz, rows, widths, name):
    return pl.pallas_call(
        functools.partial(grad_kernel, dz),
        grid_spec=pltpu.PrefetchScalarGridSpec(
            num_scalar_prefetch=1,
            grid=(1,),
            in_specs=[pl.BlockSpec(memory_space=pltpu.VMEM)] * 2,
            out_specs=[whole((rows, wide)) for wide in widths],
        ),
        out_shape=[pltpu.HBM((rows, wide), F32) for wide in widths],
        compiler_params=pltpu.CompilerParams(vmem_limit_bytes=LIMIT),
        name=name,
    )(pos, both, both_c)


def hidden_kernel(pos, hidden, gain, inv, backs, out, scratch):
    width = hidden.shape[1]
    total = jnp.zeros((hidden.shape[0], 128), F32)
    for j in range(width // 128):
        at = slice(j * 128, (j + 1) * 128)
        scaled = gain[at][None] * backs[at, :].T
        total = total + scaled * hidden[:, at].astype(F32)
        scratch[:, at] = scaled
    project = jnp.sum(total, axis=1, keepdims=True) / width
    inverse = inv[...]
    factor = inverse * inverse * inverse * project
    for j in range(width // 128):
        at = slice(j * 128, (j + 1) * 128)
        out[:, at] = (inverse * scratch[:, at] - hidden[:, at].astype(F32) * factor).astype(BF)


def adam_kernel(pos, rates, own, far, slot, first, second, *refs):
    totals, (out, first_out, second_out, ordered) = refs[:NX], refs[-4:]
    for d in range(NX):
        ordered[lax.rem(pos[1] + NX - d, NX)] = totals[d][0]
    rows = own.shape[0]
    half = rows // 2
    grad = own[...] + far[...]
    first_next = beta_first * first[...] + (1.0 - beta_first) * grad
    second_next = beta_second * second[...] + (1.0 - beta_second) * grad * grad
    first_out[...] = first_next
    second_out[...] = second_next
    snapshot = slot[...].astype(F32)
    updated = snapshot - rates[0] * (
        (first_next * rates[1]) / (jnp.sqrt(second_next * rates[2]) + adam_eps)
        + weight_decay * snapshot
    )
    left = lane_half((half, 128))
    for x in range(0, NX, 2):
        at = slice(x * 64, x * 64 + 128)
        a, b = ordered[x], ordered[x + 1]
        top = jnp.where(left, a, pltpu.roll(b, 64, 1))
        bottom = jnp.where(left, pltpu.roll(a, 64, 1), b)
        out[0, :half, at] = (mix_share * updated[:half, at] + (1.0 - mix_share) * top).astype(BF)
        out[0, half:, at] = (mix_share * updated[half:, at] + (1.0 - mix_share) * bottom).astype(BF)


def adam(pos, rates, own, far, slot, first, second, totals, held, begin):
    rows, kv = own.shape
    wide = kv // NH
    steps = far.shape[1] // wide
    skip = begin // wide
    column = pl.BlockSpec((rows, wide), lambda i, *_: (0, skip + i))
    share_block = pl.BlockSpec((1,) + totals[0].shape[1:], lambda i, *_: (skip + i, 0, 0))
    columns = [in_hbm(a) for a in (own, far, slot, first, second)]
    in_specs = [column] * 5 + [share_block] * NX + [pl.BlockSpec(memory_space=pl.ANY)] * len(held)
    in_specs[1] = pl.BlockSpec((rows, wide), lambda i, *_: (0, i))
    return pl.pallas_call(
        adam_kernel,
        grid_spec=pltpu.PrefetchScalarGridSpec(
            num_scalar_prefetch=2,
            grid=(steps,),
            in_specs=in_specs,
            out_specs=[
                pl.BlockSpec((1, rows, wide), lambda i, pos, rates: (pos[0], 0, skip + i)),
                column,
                column,
            ],
            scratch_shapes=[pltpu.VMEM((NX,) + totals[0].shape[1:], F32)],
        ),
        out_shape=[shape(held[0].shape, BF), shape((rows, kv), F32), shape((rows, kv), F32)],
        input_output_aliases={7 + NX + k: k for k in range(len(held))},
        compiler_params=pltpu.CompilerParams(vmem_limit_bytes=LIMIT),
        name="adam",
    )(pos, rates, *columns, *totals, *held)


def last_kernel(pos, rates, hidden, gain, inv, backs, own, far, slot, first, second, *refs):
    totals, (hidden_out, out, first_out, second_out, scratch, ordered) = refs[:NX], refs[-6:]
    hidden_kernel(pos, hidden, gain, inv, backs, hidden_out, scratch)
    wide = 64 * NX
    for k in range(own.shape[1] // wide):
        at = slice(k * wide, (k + 1) * wide)
        adam_kernel(
            pos,
            rates,
            *(a.at[:, at] for a in (own, far, slot, first, second)),
            *(t.at[k : k + 1] for t in totals),
            out.at[:, :, at],
            first_out.at[:, at],
            second_out.at[:, at],
            ordered,
        )


def last(pos, rates, hidden, gain, inv, backs, own, far, slot, first, second, totals, held):
    rows, kv = own.shape
    wide = far.shape[1]
    end = kv // wide - 1
    column = pl.BlockSpec((rows, wide), lambda *_: (0, end))
    share_block = pl.BlockSpec((NH * wide // kv,) + totals[0].shape[1:], lambda *_: (end, 0, 0))
    tokens = [in_hbm(a) for a in (hidden, gain, inv, backs)]
    columns = [in_hbm(a) for a in (own, far, slot, first, second)]
    return pl.pallas_call(
        last_kernel,
        grid_spec=pltpu.PrefetchScalarGridSpec(
            num_scalar_prefetch=2,
            grid=(1,),
            in_specs=[whole(a.shape) for a in tokens]
            + [column, whole(far.shape)]
            + [column] * 3
            + [share_block] * NX
            + [ANY] * 3,
            out_specs=[
                whole(hidden.shape),
                pl.BlockSpec((1, rows, wide), lambda i, pos, rates: (pos[0], 0, end)),
                column,
                column,
            ],
            scratch_shapes=[
                pltpu.VMEM(hidden.shape, F32),
                pltpu.VMEM((NX,) + totals[0].shape[1:], F32),
            ],
        ),
        out_shape=[shape(hidden.shape, BF)] + [shape(a.shape, a.dtype) for a in held],
        input_output_aliases={11 + NX + k: 1 + k for k in range(3)},
        compiler_params=pltpu.CompilerParams(vmem_limit_bytes=2 * LIMIT),
        name="last",
    )(pos, rates, *tokens, *columns, *totals, *held)


def local(
    hidden,
    key_cotangent,
    norm_gain,
    weights,
    adam_first,
    adam_second,
    inner_step,
    outer_global,
    outer_momentum,
):
    tokens, width = hidden.shape
    rows, kv = weights.shape[2:]
    frag_index = inner_step % FRAGS
    widths = [kv // 2, kv // 4, kv // 4]
    replica = lax.axis_index("replica")
    place = lax.axis_index("fsdp")
    pos = jnp.stack(
        [frag_index, replica % NX, replica // NX, place // 4, (place // 2) % 2, place % 2]
    ).astype(jnp.int32)
    counter = inner_step.astype(F32)
    rates = jnp.stack(
        [
            inner_rate * jnp.minimum(F32(1.0), counter / warmup_steps),
            1.0 / (1.0 - jnp.power(F32(beta_first), counter)),
            1.0 / (1.0 - jnp.power(F32(beta_second), counter)),
        ]
    )
    gain = norm_gain

    both, inv = call(
        norm_kernel,
        "norm",
        [pltpu.HBM((NY, width // NY + kv, tokens), BF), pltpu.HBM((tokens, 128), F32)],
        (pos, *(in_hbm(a) for a in (hidden, gain, key_cotangent))),
    )
    both = fsdp_trade(both)
    pos, inv = after(pos, inv)

    slot, *pieces = pick(pos, weights[0])
    w_z = fsdp_move(slot, 1, 0)
    pieces = [pieces[0]] + [replica_turn(pieces[d], d) for d in range(1, NX)]
    w_c = fsdp_move(slot, 0, 1)
    pos, slot = after(pos, slot)

    turned = [jnp.swapaxes(a, 1, 2) for a in (outer_global, outer_momentum)]
    packed = shape((NH, rows // 2, 128), F32)
    (totals,) = call(sum_x_kernel, "sum_x", [packed], (pos, *pieces, *turned))
    pos, totals = after(pos, totals)
    near_totals = replica_swap(totals, 0)
    w_z, totals = after(w_z, totals)
    w_zc = fsdp_move(w_z, 0, 1)
    pos, w_c, w_zc = lax.optimization_barrier((pos, w_c, w_zc))
    kept = keep(pos, weights[0])
    pos, kept = after(pos, kept)
    (totals,) = call(pair_kernel, "sum_h", [packed], (pos, totals, near_totals))
    pos, totals = after(pos, totals)
    far_totals = replica_swap(totals, 1)

    both, totals = after(both, totals)
    both_c = fsdp_move(both, 0, 1)
    backs = back_product(pos, (slot, w_z, w_c, w_zc), both)
    pos, backs = after(pos, backs)

    sums = grad_product(pos, both, both_c, 1, rows, widths, "grad_far")
    pos, *sums = lax.optimization_barrier((pos, *sums))
    (totals,) = call(pair_kernel, "sum_hh", [packed], (pos, totals, far_totals))
    pos, totals, backs, *sums = lax.optimization_barrier((pos, totals, backs, *sums))
    backs = fsdp_trade(backs).reshape(width, tokens)
    far = [fsdp_move(part, 1, 0) for part in sums]
    all_totals = [totals] + [replica_turn(totals, d) for d in range(1, NX)]
    (own,) = grad_product(pos, both, both_c, 0, rows, [kv], "grad_near")
    pos, own = after(pos, own)

    new_global, new_momentum = call(
        outer_kernel, "outer", [shape(turned[0].shape, F32)] * 2, (pos, totals, *turned)
    )
    pos, new_global = after(pos, new_global)
    held, begin = (kept,), 0
    for part in far[:-1]:
        held = adam(
            pos, rates, own, part, slot, adam_first[0], adam_second[0], all_totals, held, begin
        )
        begin += part.shape[1]
    hidden_grad, layers_out, first_next, second_next = last(
        pos,
        rates,
        hidden,
        gain,
        inv,
        backs,
        own,
        far[-1],
        slot,
        adam_first[0],
        adam_second[0],
        all_totals,
        held,
    )
    return (
        layers_out[None],
        hidden_grad,
        first_next[None],
        second_next[None],
        jnp.swapaxes(new_global, 1, 2),
        jnp.swapaxes(new_momentum, 1, 2),
    )


def solution(mesh):
    in_specs = (
        P(("replica", "fsdp"), None),
        P(("replica", "fsdp"), None),
        P(),
        P("replica", None, "fsdp", None),
        P("replica", "fsdp", None),
        P("replica", "fsdp", None),
        P(),
        P(None, "fsdp", "replica"),
        P(None, "fsdp", "replica"),
    )
    out_specs = (
        P("replica", None, "fsdp", None),
        P(("replica", "fsdp"), None),
        P("replica", "fsdp", None),
        P("replica", "fsdp", None),
        P(None, "fsdp", "replica"),
        P(None, "fsdp", "replica"),
    )
    return jax.shard_map(local, mesh=mesh, in_specs=in_specs, out_specs=out_specs, check_vma=False)
```

```python
import functools

import jax
import jax.numpy as jnp
from jax import lax
from jax.experimental import pallas as pl
from jax.experimental.pallas import tpu as pltpu
from jax.sharding import PartitionSpec as P

FRAGS = 4
NY = 4
NX = 4
NH = 4

beta_first = 0.9
beta_second = 0.95
inner_rate = 0.004
warmup_steps = 4096.0
weight_decay = 0.1
outer_rate = 0.7
outer_mom = 0.9
mix_share = 0.5
norm_eps = 1e-06
adam_eps = 1e-08

BF = jnp.bfloat16
F32 = jnp.float32
LIMIT = 20 * 1024 * 1024
MEAN_SHARE = outer_rate * (1.0 + outer_mom) / (NX * NH)


def shape(dims, dtype):
    return jax.ShapeDtypeStruct(dims, dtype)


ANY = pl.BlockSpec(memory_space=pl.ANY)


def in_hbm(array):
    return pltpu.with_memory_space_constraint(array, pltpu.HBM)


def whole(dims):
    return pl.BlockSpec(dims, lambda *_: (0,) * len(dims))


def call(kernel, name, outs, operands, scratch=()):
    return pl.pallas_call(
        kernel,
        grid_spec=pltpu.PrefetchScalarGridSpec(
            num_scalar_prefetch=1,
            grid=(1,),
            in_specs=[whole(a.shape) for a in operands[1:]],
            out_specs=[whole(o.shape) for o in outs],
            scratch_shapes=list(scratch),
        ),
        out_shape=list(outs),
        compiler_params=pltpu.CompilerParams(vmem_limit_bytes=LIMIT),
        name=name,
    )(*operands)


def fsdp_move(array, dz, dc):
    return lax.ppermute(array, "fsdp", [(i, i ^ (dz * 2 + dc)) for i in range(4 * NY)])


def fsdp_trade(array):
    groups = [[y * 4 + i for y in range(NY)] for i in range(4)]
    return lax.all_to_all(array, "fsdp", 0, 0, axis_index_groups=groups, tiled=True)


def replica_turn(array, dx):
    pairs = [(i, i // NX * NX + (i % NX + dx) % NX) for i in range(NH * NX)]
    return lax.ppermute(array, "replica", pairs)


def replica_swap(array, step):
    pairs = []
    for replica in range(NH * NX):
        for place in range(4 * NY):
            flip = (1, 3)[(step + place) % 2]
            pairs.append((replica * 4 * NY + place, (replica ^ (flip * NX)) * 4 * NY + place))
    return lax.ppermute(array, ("replica", "fsdp"), pairs)


def after(pos, done):
    return lax.optimization_barrier((pos, done))


def lane_half(block_shape):
    return lax.broadcasted_iota(jnp.int32, block_shape, 1) < 64


def pick_kernel(pos, w_ref, slot_ref, *outs):
    outs, pieces = outs[:NX], outs[NX]
    slot_ref[...] = w_ref[0]
    half = w_ref.shape[1] // 2
    left = lane_half((half, 128))
    for q in range(w_ref.shape[2] // 128):
        block = w_ref[0, :, q * 128 : (q + 1) * 128].astype(F32)
        top, bottom = block[:half], block[half:]
        h, x = 2 * q // NX, 2 * q % NX
        pieces[x, h] = jnp.where(left, top, pltpu.roll(bottom, 64, 1)).astype(BF)
        pieces[x + 1, h] = jnp.where(left, pltpu.roll(top, 64, 1), bottom).astype(BF)
    for d in range(NX):
        outs[d][...] = pieces[lax.rem(pos[1] + d, NX)]


def pick(pos, weights):
    _, rows, kv = weights.shape
    piece = (NH, rows // 2, 128)
    return pl.pallas_call(
        pick_kernel,
        grid_spec=pltpu.PrefetchScalarGridSpec(
            num_scalar_prefetch=1,
            grid=(1,),
            in_specs=[pl.BlockSpec((1, rows, kv), lambda i, pos: (pos[0], 0, 0))],
            out_specs=[whole((rows, kv))] + [whole(piece)] * NX,
            scratch_shapes=[pltpu.VMEM((NX,) + piece, BF)],
        ),
        out_shape=[shape((rows, kv), BF)] + [shape(piece, BF)] * NX,
        compiler_params=pltpu.CompilerParams(vmem_limit_bytes=LIMIT),
        name="pick",
    )(pos, in_hbm(weights))


def keep_kernel(pos, w_ref, out):
    out[...] = w_ref[...]


def keep(pos, weights):
    block = pl.BlockSpec((1,) + weights.shape[1:], lambda i, pos: (i, 0, 0))
    return pl.pallas_call(
        keep_kernel,
        grid_spec=pltpu.PrefetchScalarGridSpec(
            num_scalar_prefetch=1,
            grid=(weights.shape[0],),
            in_specs=[block],
            out_specs=block,
        ),
        out_shape=shape(weights.shape, BF),
        compiler_params=pltpu.CompilerParams(vmem_limit_bytes=LIMIT),
        name="keep",
    )(pos, in_hbm(weights))


def stepped(slot, mom, mean):
    pseudo = slot - mean
    momentum = outer_mom * mom + pseudo
    return slot - outer_rate * (pseudo + outer_mom * momentum), momentum


def sum_x_kernel(pos, a, b, c, d, glob, mom, out):
    for h in range(NH):
        total = (a[h].astype(F32) + b[h].astype(F32)) + (c[h].astype(F32) + d[h].astype(F32))
        out[h] = MEAN_SHARE * total
    updated, _ = stepped(glob[pos[0]], mom[pos[0]], 0.0)
    half = updated.shape[1] // 2
    updated = jnp.concatenate([updated[:, :half], updated[:, half:]], axis=0).T
    out[pos[2]] = out[pos[2]] + updated


def pair_kernel(pos, a, b, out):
    out[...] = a[...] + b[...]


def outer_kernel(pos, totals, glob, mom, new_glob, new_mom):
    frag = pos[0]
    updated = totals[pos[2]].T
    updated = jnp.concatenate([updated[:64], updated[64:]], axis=1)
    new_glob[...] = glob[...]
    new_mom[...] = mom[...]
    new_glob[frag] = updated
    alone, _ = stepped(glob[frag], mom[frag], 0.0)
    mean = (updated - alone) / (outer_rate * (1.0 + outer_mom))
    new_mom[frag] = stepped(glob[frag], mom[frag], mean)[1]


def norm_kernel(pos, hidden, gain, cot, out, inv_out):
    tokens, width = hidden.shape
    chunk = width // NY
    total = jnp.zeros((tokens, 128), F32)
    for j in range(width // 128):
        block = hidden[:, j * 128 : (j + 1) * 128].astype(F32)
        total = total + block * block
    mean = jnp.sum(total, axis=1, keepdims=True) / width
    inverse = lax.rsqrt(mean + norm_eps)
    inv_out[...] = jnp.broadcast_to(inverse, inv_out.shape)
    for y in range(NY):
        for j in range(chunk // 128):
            at = slice(y * chunk + j * 128, y * chunk + (j + 1) * 128)
            block = hidden[:, at].astype(F32) * inverse * gain[at][None]
            out[y, j * 128 : (j + 1) * 128, :] = block.T.astype(BF)
        for j in range(cot.shape[1] // 128):
            at = slice(j * 128, (j + 1) * 128)
            out[y, chunk + j * tokens : chunk + (j + 1) * tokens, :] = cot[:, at]


def back_kernel(pos, w0, wz, wc, wzc, both, out, w_v, turned, out_v, in_sem, out_sem):
    rows, depth = w0.shape
    tokens = both.shape[2]
    loads = []
    for k, w in enumerate((w0, wc, wz, wzc)):
        loads.append(pltpu.make_async_copy(w, w_v.at[k], in_sem.at[k]))
        loads[k].start()
    for y in range(NY):
        for j in range(depth // 128):
            cot = both[y, 4 * rows + j * tokens : 4 * rows + (j + 1) * tokens, :]
            turned[j * 128 : (j + 1) * 128, y * tokens : (y + 1) * tokens] = cot.T
    stores = []
    for k, (dz, dc) in enumerate(((0, 0), (0, 1), (1, 0), (1, 1))):
        start = (jnp.bitwise_xor(pos[4], dz) * 2 + jnp.bitwise_xor(pos[5], dc)) * rows
        at = pl.ds(pl.multiple_of(start, 32), rows)
        loads[k].wait()
        for pair in range(NY // 2):
            cot = turned[:, 2 * pair * tokens : (2 * pair + 2) * tokens]
            product = jnp.dot(w_v[k], cot, preferred_element_type=F32)
            out_v[2 * pair, at, :] = product[:, :tokens]
            out_v[2 * pair + 1, at, :] = product[:, tokens:]
        stores.append(pltpu.make_async_copy(out_v.at[:, at, :], out.at[:, at, :], out_sem.at[k]))
        stores[k].start()
    for copy in stores:
        copy.wait()


def back_product(pos, weights, both):
    rows, kv = weights[0].shape
    tokens = both.shape[2]
    return pl.pallas_call(
        back_kernel,
        grid_spec=pltpu.PrefetchScalarGridSpec(
            num_scalar_prefetch=1,
            grid=(1,),
            in_specs=[ANY] * 4 + [pl.BlockSpec(memory_space=pltpu.VMEM)],
            out_specs=ANY,
            scratch_shapes=[
                pltpu.VMEM((4, rows, kv), BF),
                pltpu.VMEM((kv, NY * tokens), BF),
                pltpu.VMEM((NY, 4 * rows, tokens), F32),
                pltpu.SemaphoreType.DMA((4,)),
                pltpu.SemaphoreType.DMA((4,)),
            ],
        ),
        out_shape=pltpu.HBM((NY, 4 * rows, tokens), F32),
        compiler_params=pltpu.CompilerParams(vmem_limit_bytes=LIMIT),
        name="back_product",
    )(pos, *(in_hbm(w) for w in weights), both)


def grad_kernel(dz, pos, mine, theirs, *outs):
    rows = outs[0].shape[0]
    tokens = mine.shape[2]
    start = (jnp.bitwise_xor(pos[4], dz) * 2 + pos[5]) * rows
    at = pl.ds(pl.multiple_of(start, 32), rows)
    left = jnp.concatenate([both[y, at, :] for both in (mine, theirs) for y in range(NY)], axis=1)
    b = 0
    for out in outs:
        for j in range(out.shape[1] // 256):
            columns = []
            for _ in range(2):
                lines = slice(4 * rows + b * tokens, 4 * rows + (b + 1) * tokens)
                blocks = [both[y, lines, :] for both in (mine, theirs) for y in range(NY)]
                columns.append(jnp.concatenate(blocks, axis=0))
                b += 1
            out[:, j * 256 : (j + 1) * 256] = jnp.dot(
                left, jnp.concatenate(columns, axis=1), preferred_element_type=F32
            )


def grad_product(pos, both, both_c, dz, rows, widths, name):
    return pl.pallas_call(
        functools.partial(grad_kernel, dz),
        grid_spec=pltpu.PrefetchScalarGridSpec(
            num_scalar_prefetch=1,
            grid=(1,),
            in_specs=[pl.BlockSpec(memory_space=pltpu.VMEM)] * 2,
            out_specs=[whole((rows, wide)) for wide in widths],
        ),
        out_shape=[pltpu.HBM((rows, wide), F32) for wide in widths],
        compiler_params=pltpu.CompilerParams(vmem_limit_bytes=LIMIT),
        name=name,
    )(pos, both, both_c)


def hidden_kernel(pos, hidden, gain, inv, backs, out, scratch):
    width = hidden.shape[1]
    total = jnp.zeros((hidden.shape[0], 128), F32)
    for j in range(width // 128):
        at = slice(j * 128, (j + 1) * 128)
        scaled = gain[at][None] * backs[at, :].T
        total = total + scaled * hidden[:, at].astype(F32)
        scratch[:, at] = scaled
    project = jnp.sum(total, axis=1, keepdims=True) / width
    inverse = inv[...]
    factor = inverse * inverse * inverse * project
    for j in range(width // 128):
        at = slice(j * 128, (j + 1) * 128)
        out[:, at] = (inverse * scratch[:, at] - hidden[:, at].astype(F32) * factor).astype(BF)


def adam_kernel(pos, rates, own, far, slot, first, second, *refs):
    totals, (out, first_out, second_out, ordered) = refs[:NX], refs[-4:]
    for d in range(NX):
        ordered[lax.rem(pos[1] + NX - d, NX)] = totals[d][0]
    rows = own.shape[0]
    half = rows // 2
    grad = own[...] + far[...]
    first_next = beta_first * first[...] + (1.0 - beta_first) * grad
    second_next = beta_second * second[...] + (1.0 - beta_second) * grad * grad
    first_out[...] = first_next
    second_out[...] = second_next
    snapshot = slot[...].astype(F32)
    updated = snapshot - rates[0] * (
        (first_next * rates[1]) / (jnp.sqrt(second_next * rates[2]) + adam_eps)
        + weight_decay * snapshot
    )
    left = lane_half((half, 128))
    for x in range(0, NX, 2):
        at = slice(x * 64, x * 64 + 128)
        a, b = ordered[x], ordered[x + 1]
        top = jnp.where(left, a, pltpu.roll(b, 64, 1))
        bottom = jnp.where(left, pltpu.roll(a, 64, 1), b)
        out[0, :half, at] = (mix_share * updated[:half, at] + (1.0 - mix_share) * top).astype(BF)
        out[0, half:, at] = (mix_share * updated[half:, at] + (1.0 - mix_share) * bottom).astype(BF)


def adam(pos, rates, own, far, slot, first, second, totals, held, begin):
    rows, kv = own.shape
    wide = kv // NH
    steps = far.shape[1] // wide
    skip = begin // wide
    column = pl.BlockSpec((rows, wide), lambda i, *_: (0, skip + i))
    share_block = pl.BlockSpec((1,) + totals[0].shape[1:], lambda i, *_: (skip + i, 0, 0))
    columns = [in_hbm(a) for a in (own, far, slot, first, second)]
    in_specs = [column] * 5 + [share_block] * NX + [pl.BlockSpec(memory_space=pl.ANY)] * len(held)
    in_specs[1] = pl.BlockSpec((rows, wide), lambda i, *_: (0, i))
    return pl.pallas_call(
        adam_kernel,
        grid_spec=pltpu.PrefetchScalarGridSpec(
            num_scalar_prefetch=2,
            grid=(steps,),
            in_specs=in_specs,
            out_specs=[
                pl.BlockSpec((1, rows, wide), lambda i, pos, rates: (pos[0], 0, skip + i)),
                column,
                column,
            ],
            scratch_shapes=[pltpu.VMEM((NX,) + totals[0].shape[1:], F32)],
        ),
        out_shape=[shape(held[0].shape, BF), shape((rows, kv), F32), shape((rows, kv), F32)],
        input_output_aliases={7 + NX + k: k for k in range(len(held))},
        compiler_params=pltpu.CompilerParams(vmem_limit_bytes=LIMIT),
        name="adam",
    )(pos, rates, *columns, *totals, *held)


def last_kernel(pos, rates, hidden, gain, inv, backs, own, far, slot, first, second, *refs):
    totals, (hidden_out, out, first_out, second_out, scratch, ordered) = refs[:NX], refs[-6:]
    hidden_kernel(pos, hidden, gain, inv, backs, hidden_out, scratch)
    wide = 64 * NX
    for k in range(own.shape[1] // wide):
        at = slice(k * wide, (k + 1) * wide)
        adam_kernel(
            pos,
            rates,
            *(a.at[:, at] for a in (own, far, slot, first, second)),
            *(t.at[k : k + 1] for t in totals),
            out.at[:, :, at],
            first_out.at[:, at],
            second_out.at[:, at],
            ordered,
        )


def last(pos, rates, hidden, gain, inv, backs, own, far, slot, first, second, totals, held):
    rows, kv = own.shape
    wide = far.shape[1]
    end = kv // wide - 1
    column = pl.BlockSpec((rows, wide), lambda *_: (0, end))
    share_block = pl.BlockSpec((NH * wide // kv,) + totals[0].shape[1:], lambda *_: (end, 0, 0))
    tokens = [in_hbm(a) for a in (hidden, gain, inv, backs)]
    columns = [in_hbm(a) for a in (own, far, slot, first, second)]
    return pl.pallas_call(
        last_kernel,
        grid_spec=pltpu.PrefetchScalarGridSpec(
            num_scalar_prefetch=2,
            grid=(1,),
            in_specs=[whole(a.shape) for a in tokens]
            + [column, whole(far.shape)]
            + [column] * 3
            + [share_block] * NX
            + [ANY] * 3,
            out_specs=[
                whole(hidden.shape),
                pl.BlockSpec((1, rows, wide), lambda i, pos, rates: (pos[0], 0, end)),
                column,
                column,
            ],
            scratch_shapes=[
                pltpu.VMEM(hidden.shape, F32),
                pltpu.VMEM((NX,) + totals[0].shape[1:], F32),
            ],
        ),
        out_shape=[shape(hidden.shape, BF)] + [shape(a.shape, a.dtype) for a in held],
        input_output_aliases={11 + NX + k: 1 + k for k in range(3)},
        compiler_params=pltpu.CompilerParams(vmem_limit_bytes=2 * LIMIT),
        name="last",
    )(pos, rates, *tokens, *columns, *totals, *held)


def local(
    hidden,
    key_cotangent,
    norm_gain,
    weights,
    adam_first,
    adam_second,
    inner_step,
    outer_global,
    outer_momentum,
):
    tokens, width = hidden.shape
    rows, kv = weights.shape[2:]
    frag_index = inner_step % FRAGS
    widths = [kv // 2, kv // 4, kv // 4]
    replica = lax.axis_index("replica")
    place = lax.axis_index("fsdp")
    pos = jnp.stack(
        [frag_index, replica % NX, replica // NX, place // 4, (place // 2) % 2, place % 2]
    ).astype(jnp.int32)
    counter = inner_step.astype(F32)
    rates = jnp.stack(
        [
            inner_rate * jnp.minimum(F32(1.0), counter / warmup_steps),
            1.0 / (1.0 - jnp.power(F32(beta_first), counter)),
            1.0 / (1.0 - jnp.power(F32(beta_second), counter)),
        ]
    )
    gain = norm_gain

    both, inv = call(
        norm_kernel,
        "norm",
        [pltpu.HBM((NY, width // NY + kv, tokens), BF), pltpu.HBM((tokens, 128), F32)],
        (pos, *(in_hbm(a) for a in (hidden, gain, key_cotangent))),
    )
    both = fsdp_trade(both)
    pos, inv = after(pos, inv)

    slot, *pieces = pick(pos, weights[0])
    w_z = fsdp_move(slot, 1, 0)
    pieces = [pieces[0]] + [replica_turn(pieces[d], d) for d in range(1, NX)]
    w_c = fsdp_move(slot, 0, 1)
    pos, slot = after(pos, slot)

    turned = [jnp.swapaxes(a, 1, 2) for a in (outer_global, outer_momentum)]
    packed = shape((NH, rows // 2, 128), F32)
    (totals,) = call(sum_x_kernel, "sum_x", [packed], (pos, *pieces, *turned))
    pos, totals = after(pos, totals)
    near_totals = replica_swap(totals, 0)
    w_z, totals = after(w_z, totals)
    w_zc = fsdp_move(w_z, 0, 1)
    pos, w_c, w_zc = lax.optimization_barrier((pos, w_c, w_zc))
    kept = keep(pos, weights[0])
    pos, kept = after(pos, kept)
    (totals,) = call(pair_kernel, "sum_h", [packed], (pos, totals, near_totals))
    pos, totals = after(pos, totals)
    far_totals = replica_swap(totals, 1)

    both, totals = after(both, totals)
    both_c = fsdp_move(both, 0, 1)
    backs = back_product(pos, (slot, w_z, w_c, w_zc), both)
    pos, backs = after(pos, backs)

    sums = grad_product(pos, both, both_c, 1, rows, widths, "grad_far")
    pos, far_totals, backs, *sums = lax.optimization_barrier((pos, far_totals, backs, *sums))
    backs = fsdp_trade(backs).reshape(width, tokens)
    (totals,) = call(pair_kernel, "sum_hh", [packed], (pos, totals, far_totals))
    pos, totals, *sums = lax.optimization_barrier((pos, totals, *sums))
    far = [fsdp_move(part, 1, 0) for part in sums[:-1]]
    all_totals = [totals] + [replica_turn(totals, d) for d in range(1, NX)]
    (own,) = grad_product(pos, both, both_c, 0, rows, [kv], "grad_near")
    pos, own, sums[-1] = lax.optimization_barrier((pos, own, sums[-1]))
    far.append(fsdp_move(sums[-1], 1, 0))

    new_global, new_momentum = call(
        outer_kernel, "outer", [shape(turned[0].shape, F32)] * 2, (pos, totals, *turned)
    )
    pos, new_global = after(pos, new_global)
    held, begin = (kept,), 0
    for part in far[:-1]:
        held = adam(
            pos, rates, own, part, slot, adam_first[0], adam_second[0], all_totals, held, begin
        )
        begin += part.shape[1]
    hidden_grad, layers_out, first_next, second_next = last(
        pos,
        rates,
        hidden,
        gain,
        inv,
        backs,
        own,
        far[-1],
        slot,
        adam_first[0],
        adam_second[0],
        all_totals,
        held,
    )
    return (
        layers_out[None],
        hidden_grad,
        first_next[None],
        second_next[None],
        jnp.swapaxes(new_global, 1, 2),
        jnp.swapaxes(new_momentum, 1, 2),
    )


def solution(mesh):
    in_specs = (
        P(("replica", "fsdp"), None),
        P(("replica", "fsdp"), None),
        P(),
        P("replica", None, "fsdp", None),
        P("replica", "fsdp", None),
        P("replica", "fsdp", None),
        P(),
        P(None, "fsdp", "replica"),
        P(None, "fsdp", "replica"),
    )
    out_specs = (
        P("replica", None, "fsdp", None),
        P(("replica", "fsdp"), None),
        P("replica", "fsdp", None),
        P("replica", "fsdp", None),
        P(None, "fsdp", "replica"),
        P(None, "fsdp", "replica"),
    )
    return jax.shard_map(local, mesh=mesh, in_specs=in_specs, out_specs=out_specs, check_vma=False)
```
